32 devices in a mesh: row: 8 (over y, x, core), col: 4 (over z).
Axes of the slice: x: 2, y: 2, z: 4, core: 2. Of those that a mesh axis runs over, the one named last changes fastest.
Arguments:
- matrix: float32 [24576, 2048], P('row', 'col'), may hold values from -6 to 6
Outputs:
- top_rows: float32 [2048, 256], P(('col', 'row'))
- remainder: float32 [24576, 2048], P('row', 'col')
The draws below stay inside these ranges and needn't reach their ends.
All inputs are finite; a program needn't handle non-finite values.
Results may differ from the reference program's by a relative error of at most 0.00013.
Values sent between devices are 32-bit elements; how exact they have to be, the bound alone decides.
No kernel may reach another device: no remote copies, remote signals or barrier semaphores. Data moves between devices by JAX's collectives and lax.ppermute only.
A program may use at most 64 MiB of HBM per device.

```python
import jax
import jax.numpy as jnp
from jax import lax

PANEL = 256
M = 24576
N = 2048


def block_scale(stream_key, dims, shards, least, top_value):
    level = 1.0
    for position, parts in shards:
        steps = jax.random.uniform(jax.random.fold_in(jax.random.fold_in(stream_key, 6), position), (parts,), jnp.float32, least / len(shards), top_value / len(shards))
        level = level * jnp.repeat(jnp.exp(steps), dims[position] // parts).reshape((-1,) + (1,) * (len(dims) - 1 - position))
    return level


def scatter_about(own_key, shape, scale, reach, shards=(), dtype=jnp.bfloat16):
    factor_of = block_scale(own_key, shape, shards, -0.22, 0.18) if shards else 1.0
    array = jax.random.normal(own_key, shape, jnp.float32) * scale * factor_of
    return jnp.minimum(jnp.maximum(array, -reach), reach).astype(dtype)


def setup_inputs(seed: int = 0) -> dict:
    key_list = jax.random.split(jax.random.key(seed), 2)
    matrix = scatter_about(key_list[0], (M, N), 1.0, 6.0, ((0, 8), (1, 4)), jnp.float32)
    return {"matrix": matrix}


def reference(matrix):
    highest = lax.Precision.HIGHEST
    panel_cols = matrix[:, :PANEL]
    gram_matrix = jnp.dot(panel_cols.T.astype(jnp.float32), panel_cols.astype(jnp.float32), precision=highest, preferred_element_type=jnp.float32)
    lower_factor = jnp.linalg.cholesky(gram_matrix)
    products = jnp.dot(matrix.T.astype(jnp.float32), panel_cols.astype(jnp.float32), precision=highest, preferred_element_type=jnp.float32)
    top_rows = lax.linalg.triangular_solve(lower_factor, products, left_side=False, lower=True, transpose_a=True)
    coeffs = lax.linalg.triangular_solve(lower_factor, top_rows, left_side=False, lower=True)
    remainder = matrix - jnp.dot(panel_cols.astype(jnp.float32), coeffs.T.astype(jnp.float32), precision=highest, preferred_element_type=jnp.float32)
    return (top_rows, remainder)
```

```python
import jax
import jax.numpy as jnp
from jax import lax
from jax.experimental import pallas as pl
from jax.experimental.pallas import tpu as pltpu
from jax.sharding import PartitionSpec as P

PANEL = 256
CHUNKS = 8
AHEAD = 2
BLOCK = 32
VMEM = 48 * 1024 * 1024
HIGHEST = lax.Precision.HIGHEST
F32, BF16 = jnp.float32, jnp.bfloat16
ANY = pl.BlockSpec(memory_space=pl.ANY)
SMEM = pl.BlockSpec(memory_space=pltpu.SMEM)


def whole(shape):
    return pl.BlockSpec(shape, lambda *i: (0,) * len(shape))


def params():
    return pltpu.CompilerParams(vmem_limit_bytes=VMEM)


def cost(flops, nbytes):
    return pl.CostEstimate(flops=flops, bytes_accessed=nbytes, transcendentals=0)


def split(x):
    hi = x.astype(BF16)
    return hi, (x - hi.astype(F32)).astype(BF16)


def dot(a, b, dims, precision=None):
    return lax.dot_general(
        a, b, (dims, ((), ())), precision=precision, preferred_element_type=F32
    )


def pack(matrix, chunk, rows, after):
    steps = 2

    def body(*refs):
        refs[-1][...] = refs[0][...]

    return pl.pallas_call(
        body,
        grid=(steps,),
        in_specs=[pl.BlockSpec((rows // steps, PANEL), lambda i: (chunk * steps + i, 0))]
        + [ANY] * len(after),
        out_specs=pl.BlockSpec((rows // steps, PANEL), lambda i: (i, 0)),
        out_shape=jax.ShapeDtypeStruct((rows, PANEL), F32),
        cost_estimate=cost(0, 8 * rows * PANEL),
        name=f"pack{chunk}",
    )(matrix, *after)


def gram_part(col, matrix):
    rows = matrix.shape[0]
    tile = rows // 4

    def body(col_ref, panel, out):
        @pl.when(col_ref[0] == 0)
        def _():
            @pl.when(pl.program_id(0) == 0)
            def _():
                out[...] = jnp.zeros_like(out)

            x = panel[...]
            out[...] += dot(x, x, ((0,), (0,)), HIGHEST)

    return pl.pallas_call(
        body,
        grid=(4,),
        in_specs=[SMEM, pl.BlockSpec((tile, PANEL), lambda i: (i, 0))],
        out_specs=whole((PANEL, PANEL)),
        out_shape=jax.ShapeDtypeStruct((PANEL, PANEL), F32),
        compiler_params=params(),
        cost_estimate=cost(12 * rows * PANEL * PANEL, 4 * rows * PANEL),
        name="gram",
    )(col, matrix)


def eliminate(col, state, block, after):
    first, last = block * BLOCK, (block + 1) * BLOCK
    width = 2 * PANEL

    def body(col_ref, src, *rest):
        out = rest[-1]

        @pl.when(col_ref[0] == 0)
        def _():
            if block == 0:
                row = lax.broadcasted_iota(jnp.int32, (PANEL, PANEL), 0)
                lane = lax.broadcasted_iota(jnp.int32, (PANEL, PANEL), 1)
                out[:, :PANEL] = src[...]
                out[:, PANEL:] = (row == lane).astype(F32)
            else:
                out[...] = src[...]
            row = lax.broadcasted_iota(jnp.int32, (BLOCK, BLOCK), 0)
            lane = lax.broadcasted_iota(jnp.int32, (BLOCK, BLOCK), 1)
            work = jnp.concatenate(
                [out[first:last, first:last], (row == lane).astype(F32)], axis=1
            )
            below = lax.broadcasted_iota(jnp.int32, (BLOCK, 2 * BLOCK), 0)
            scale = jnp.zeros((BLOCK, 2 * BLOCK), F32)
            for i in range(BLOCK):
                column = jnp.broadcast_to(work[:, i : i + 1], work.shape)
                pivot = column[i : i + 1, :]
                scale = jnp.where(below == i, pivot, scale)
                factor = jnp.where(below > i, column / pivot, 0.0)
                work = work - factor * work[i : i + 1, :]
            root = lax.rsqrt(scale)
            root = root * (1.5 - 0.5 * scale * root * root)
            inverse = (work * root)[:, BLOCK:]
            rows = dot(inverse, out[first:last, :], ((1,), (0,)), HIGHEST)
            out[first:last, :] = rows
            if last < PANEL:
                out[last:, :] -= dot(rows[:, last:PANEL], rows, ((0,), (0,)), HIGHEST)

    return pl.pallas_call(
        body,
        in_specs=[SMEM, whole(state.shape)] + [ANY] * len(after),
        out_specs=whole((PANEL, width)),
        out_shape=jax.ShapeDtypeStruct((PANEL, width), F32),
        grid=(1,),
        input_output_aliases={1: 0} if block else {},
        compiler_params=params(),
        cost_estimate=cost(12 * BLOCK * PANEL * width, 8 * PANEL * width),
        name=f"eliminate{block}",
    )(col, state, *after)


def consume(col, matrix, hops, chunk, before):
    rows, width = hops[0].shape[0], matrix.shape[1]
    last = chunk == CHUNKS - 1

    def body(col_ref, block, *refs):
        sources, rest = refs[: len(hops)], refs[len(hops) :]
        if chunk:
            total, _, out, halves, held, sem = rest
        else:
            out, halves, held, sem = rest
        for h, source in enumerate(sources):

            @pl.when(col_ref[0] == h)
            def _():
                copy = pltpu.make_async_copy(source, held, sem)
                copy.start()
                copy.wait()

        high, low = split(held[...])
        halves[:, :PANEL] = high
        halves[:, PANEL:] = low
        a_high, a_low = split(block[...])
        dims = ((0,), (0,))
        value = dot(high, a_high, dims) + dot(low, a_high, dims) + dot(high, a_low, dims)
        if chunk:
            value += total[...]
        out[...] = value.T if last else value

    total_shape = (width, PANEL) if last else (PANEL, width)
    out_shape = (
        jax.ShapeDtypeStruct(total_shape, F32),
        jax.ShapeDtypeStruct((matrix.shape[0], 2 * PANEL), BF16),
    )
    n = 2 + len(hops)
    return pl.pallas_call(
        body,
        grid=(1,),
        in_specs=[SMEM, pl.BlockSpec((rows, width), lambda i: (chunk, 0))]
        + [ANY] * len(hops)
        + ([whole((PANEL, width)), ANY] if chunk else []),
        out_specs=(
            whole(total_shape),
            pl.BlockSpec((rows, 2 * PANEL), lambda i: (chunk, 0)),
        ),
        out_shape=out_shape,
        input_output_aliases={n + 1: 1} if chunk else {},
        scratch_shapes=[pltpu.VMEM((rows, PANEL), F32), pltpu.SemaphoreType.DMA(())],
        compiler_params=params(),
        cost_estimate=cost(
            6 * rows * PANEL * width, 4 * rows * (2 * PANEL + width) + 8 * PANEL * width
        ),
        name=f"consume{chunk}",
    )(col, matrix, *hops, *before)


def solve(col, parts, hops):
    n, rows, _ = parts.shape

    def body(col_ref, parts_ref, *refs):
        sources, (top, coeffs, held, sem) = refs[: len(hops)], refs[len(hops) :]
        for h, source in enumerate(sources):

            @pl.when(col_ref[0] == h)
            def _():
                copy = pltpu.make_async_copy(source, held, sem)
                copy.start()
                copy.wait()

        total = parts_ref[0]
        for p in range(1, n):
            total += parts_ref[p]
        inverse = held[...]
        value = dot(total, inverse, ((1,), (1,)), HIGHEST)
        top[...] = value
        coeffs[...] = dot(value, inverse, ((1,), (0,)), HIGHEST)

    return pl.pallas_call(
        body,
        grid=(1,),
        in_specs=[SMEM, whole(parts.shape)] + [ANY] * len(hops),
        out_specs=(whole((rows, PANEL)),) * 2,
        out_shape=(jax.ShapeDtypeStruct((rows, PANEL), F32),) * 2,
        scratch_shapes=[pltpu.VMEM((PANEL, PANEL), F32), pltpu.SemaphoreType.DMA(())],
        compiler_params=params(),
        cost_estimate=cost(24 * rows * PANEL * PANEL, 4 * PANEL * PANEL),
        name="solve",
    )(col, parts, *hops)


def subtract(matrix, halves, coeffs):
    rows, width = matrix.shape
    tile = rows // 12

    def body(a, p, c, out, c_high, c_low):
        @pl.when(pl.program_id(0) == 0)
        def _():
            c_high[...], c_low[...] = split(c[...])

        high, low = p[:, :PANEL], p[:, PANEL:]
        dims = ((1,), (1,))
        out[...] = a[...] - (
            dot(high, c_high[...], dims) + dot(low, c_high[...], dims) + dot(high, c_low[...], dims)
        )

    return pl.pallas_call(
        body,
        grid=(12,),
        in_specs=[
            pl.BlockSpec((tile, width), lambda i: (i, 0)),
            pl.BlockSpec((tile, 2 * PANEL), lambda i: (i, 0)),
            whole((width, PANEL)),
        ],
        out_specs=pl.BlockSpec((tile, width), lambda i: (i, 0)),
        out_shape=jax.ShapeDtypeStruct((rows, width), F32),
        scratch_shapes=[pltpu.VMEM((width, PANEL), BF16)] * 2,
        compiler_params=params(),
        cost_estimate=cost(6 * rows * PANEL * width, 8 * rows * (width + PANEL)),
        name="subtract",
    )(matrix, halves, coeffs)


def program(n_row, n_col):
    def down(x):
        hops = [x]
        for h in range(1, n_col):
            hops.append(lax.ppermute(hops[-1], "col", [(h - 1, h)]))
        return hops

    def shards(matrix):
        rows, width = matrix.shape
        col = lax.axis_index("col").astype(jnp.int32).reshape(1)
        size = rows // CHUNKS
        blocks = PANEL // BLOCK
        chain = []
        state = None
        done = 0
        gram = None
        for k in range(CHUNKS):
            after = [chain[k - AHEAD][1 % n_col]] if k >= AHEAD else []
            if k >= AHEAD + 1 and done < blocks:
                for _ in range(2 if k >= CHUNKS - 2 else 1):
                    state = eliminate(col, gram if state is None else state, done, after[:1])
                    done += 1
                after.append(state)
            chain.append(down(pack(matrix, k, size, after)))
            if k == AHEAD - 1:
                parts = gram_part(col, matrix).reshape(n_row, PANEL // n_row, PANEL)
                mine = lax.all_to_all(parts, "row", 0, 0).sum(0)
                gram = lax.all_gather(mine, "row", axis=0, tiled=True)
        while done < blocks:
            state = eliminate(col, state, done, [chain[-1][1 % n_col]] if done == blocks - 1 else [])
            done += 1
        inverse = down(state[:, PANEL:])
        before = ()
        for k in range(CHUNKS):
            before = consume(col, matrix, chain[k], k, before)
        products, halves = before
        parts = lax.all_to_all(products.reshape(n_row, width // n_row, PANEL), "row", 0, 0)
        top_rows, coeffs = solve(col, parts, inverse)
        coeffs = lax.all_gather(coeffs, "row", axis=0, tiled=True)
        return top_rows, subtract(matrix, halves, coeffs)

    return shards


def solution(mesh):
    return jax.shard_map(
        program(mesh.shape["row"], mesh.shape["col"]),
        mesh=mesh,
        in_specs=(P("row", "col"),),
        out_specs=(P(("col", "row"), None), P("row", "col")),
        check_vma=False,
    )
```

```python
import jax
import jax.numpy as jnp
from jax import lax
from jax.experimental import pallas as pl
from jax.experimental.pallas import tpu as pltpu
from jax.sharding import PartitionSpec as P

PANEL = 256
CHUNKS = 12
LAG = 2
BLOCK = 32
HIGHEST = lax.Precision.HIGHEST
F32, BF16 = jnp.float32, jnp.bfloat16
ANY = pl.BlockSpec(memory_space=pl.ANY)
SMEM = pl.BlockSpec(memory_space=pltpu.SMEM)
VMEM = pl.BlockSpec(memory_space=pltpu.VMEM)


def params(mib):
    return pltpu.CompilerParams(vmem_limit_bytes=mib * 1024 * 1024)


def small():
    return pl.CostEstimate(flops=1, bytes_accessed=1, transcendentals=0)


def shape(*dims, dtype=F32):
    return jax.ShapeDtypeStruct(dims, dtype)


def split(x):
    hi = x.astype(BF16)
    return hi, (x - hi.astype(F32)).astype(BF16)


def dot(a, b, dims, precision=None):
    return lax.dot_general(
        a, b, (dims, ((), ())), precision=precision, preferred_element_type=F32
    )


def pack(matrix):
    rows = matrix.shape[0] // CHUNKS

    def body(source, *refs):
        outs, sems = refs[:CHUNKS], refs[CHUNKS]
        copies = [
            pltpu.make_async_copy(
                source.at[pl.ds(k * rows, rows), pl.ds(0, PANEL)], out, sems.at[k]
            )
            for k, out in enumerate(outs)
        ]
        for copy in copies:
            copy.start()
        for copy in copies:
            copy.wait()

    return pl.pallas_call(
        body,
        in_specs=[ANY],
        out_specs=(VMEM,) * CHUNKS,
        out_shape=(shape(rows, PANEL),) * CHUNKS,
        scratch_shapes=[pltpu.SemaphoreType.DMA((CHUNKS,))],
        compiler_params=params(5),
        cost_estimate=small(),
        name="pack",
    )(matrix)


def gate(x, *after):
    def body(*refs):
        pass

    return pl.pallas_call(
        body,
        in_specs=[ANY] * (1 + len(after)),
        out_specs=ANY,
        out_shape=shape(*x.shape, dtype=x.dtype),
        input_output_aliases={0: 0},
        compiler_params=params(1),
        cost_estimate=small(),
        name="gate",
    )(x, *after)


def fill(place, received, own, *after):
    def body(place_ref, _, own_ref, *refs):
        @pl.when(place_ref[0] == 0)
        def _():
            source = own_ref.at[:, pl.ds(own.shape[1] - PANEL, PANEL)]
            copy = pltpu.make_async_copy(source, refs[-2], refs[-1])
            copy.start()
            copy.wait()

    return pl.pallas_call(
        body,
        in_specs=[SMEM] + [ANY] * (2 + len(after)),
        out_specs=ANY,
        out_shape=shape(*received.shape),
        input_output_aliases={1: 0},
        scratch_shapes=[pltpu.SemaphoreType.DMA(())],
        compiler_params=params(1),
        cost_estimate=small(),
        name="fill",
    )(place, received, own, *after)


def halve(total, place_ref, keep, give, pairs):
    size = total.shape[0] // (2 * pairs)
    core = place_ref[1] % 2
    for k in range(pairs):
        here = slice(k * size, (k + 1) * size)
        mine = pl.multiple_of((2 * k + core) * size, size)
        other = pl.multiple_of((2 * k + 1 - core) * size, size)
        keep[here, :] = total[pl.ds(mine, size), :]
        give[here, :] = total[pl.ds(other, size), :]


def spread(place, keep, got, pairs):
    size = keep.shape[0] // pairs

    def body(place_ref, keep_ref, got_ref, *outs):
        chip = place_ref[1] // 2
        for j, out in enumerate(outs):
            here = pl.ds(pl.multiple_of((chip ^ j) * size, size), size)
            out[...] = keep_ref[here, :] + got_ref[here, :]

    return pl.pallas_call(
        body,
        in_specs=[SMEM, VMEM, VMEM],
        out_specs=(VMEM,) * pairs,
        out_shape=(shape(size, PANEL),) * pairs,
        compiler_params=params(4),
        cost_estimate=small(),
        name="spread",
    )(place, keep, got)


def add(parts):
    def body(*refs):
        total = refs[0][...]
        for ref in refs[1:-1]:
            total += ref[...]
        refs[-1][...] = total

    return pl.pallas_call(
        body,
        in_specs=[VMEM] * len(parts),
        out_specs=VMEM,
        out_shape=shape(*parts[0].shape),
        compiler_params=params(2),
        cost_estimate=small(),
        name="add",
    )(*parts)


def gram_part(place, chunks, pairs):
    def body(place_ref, *refs):
        sources, (keep, give, held) = refs[:-3], refs[-3:]

        @pl.when(place_ref[0] == 0)
        def _():
            total = jnp.zeros((PANEL, PANEL), F32)
            for ref in sources:
                x = ref[...]
                total += dot(x, x, ((0,), (0,)), HIGHEST)
            held[...] = total
            halve(held, place_ref, keep, give, pairs)

    return pl.pallas_call(
        body,
        in_specs=[SMEM] + [VMEM] * len(chunks),
        out_specs=(VMEM, VMEM),
        out_shape=(shape(PANEL // 2, PANEL),) * 2,
        scratch_shapes=[pltpu.VMEM((PANEL, PANEL), F32)],
        compiler_params=params(8),
        cost_estimate=small(),
        name="gram",
    )(place, *chunks)


def eliminate(col, state, block):
    first, last = block * BLOCK, (block + 1) * BLOCK
    width = 2 * PANEL

    def body(col_ref, src, out):
        @pl.when(col_ref[0] == 0)
        def _():
            if block == 0:
                row = lax.broadcasted_iota(jnp.int32, (PANEL, PANEL), 0)
                lane = lax.broadcasted_iota(jnp.int32, (PANEL, PANEL), 1)
                out[:, :PANEL] = src[...]
                out[:, PANEL:] = (row == lane).astype(F32)
            else:
                out[...] = src[...]
            row = lax.broadcasted_iota(jnp.int32, (BLOCK, BLOCK), 0)
            lane = lax.broadcasted_iota(jnp.int32, (BLOCK, BLOCK), 1)
            work = jnp.concatenate(
                [out[first:last, first:last], (row == lane).astype(F32)], axis=1
            )
            below = lax.broadcasted_iota(jnp.int32, (BLOCK, 2 * BLOCK), 0)
            scale = jnp.zeros((BLOCK, 2 * BLOCK), F32)
            for i in range(0, BLOCK, 2):
                column = jnp.broadcast_to(work[:, i : i + 1], work.shape)
                follow = jnp.broadcast_to(work[:, i + 1 : i + 2], work.shape)
                upper, lower = work[i : i + 1, :], work[i + 1 : i + 2, :]
                pivot, cross = column[i : i + 1, :], column[i + 1 : i + 2, :]
                inverse = 1.0 / pivot
                ratio = cross * inverse
                second = follow[i + 1 : i + 2, :] - ratio * follow[i : i + 1, :]
                factor = jnp.where(below > i, column * inverse, 0.0)
                follow = follow - factor * follow[i : i + 1, :]
                after = jnp.where(below > i + 1, follow * (1.0 / second), 0.0)
                lower = lower - ratio * upper
                work = work - factor * upper - after * lower
                scale = jnp.where(below == i, pivot, jnp.where(below == i + 1, second, scale))
            root = lax.rsqrt(scale)
            root = root * (1.5 - 0.5 * scale * root * root)
            rows = dot((work * root)[:, BLOCK:], out[first:last, :], ((1,), (0,)), HIGHEST)
            out[first:last, :] = rows
            if last < PANEL:
                left, right = last // 128 * 128, PANEL + -(-last // 128) * 128
                out[last:, left:right] -= dot(
                    rows[:, last:PANEL], rows[:, left:right], ((0,), (0,)), HIGHEST
                )

    return pl.pallas_call(
        body,
        in_specs=[SMEM, VMEM],
        out_specs=VMEM,
        out_shape=shape(PANEL, width),
        input_output_aliases={1: 0} if block else {},
        compiler_params=params(8),
        cost_estimate=small(),
        name=f"eliminate{block}",
    )(col, state)


def consume(place, matrix, sent, step, before, pairs):
    rows, width = sent.shape[0], matrix.shape[1]

    def body(place_ref, block, source, *refs):
        if pairs:
            total, _, keep, give, halves, held, sem, turned = refs
        elif step:
            total, _, out, halves, held, sem = refs
        else:
            out, halves, held, sem = refs
        chunk = step - LAG * place_ref[0]
        valid = (chunk >= 0) & (chunk < CHUNKS)

        def part():
            here = pl.ds(pl.multiple_of(chunk * rows, rows), rows)
            high, low = split(source[...])
            held[:, :PANEL] = high
            held[:, PANEL:] = low
            copy = pltpu.make_async_copy(held, halves.at[here, :], sem)
            copy.start()
            a_high, a_low = split(block[here, :])
            dims = ((0,), (0,))
            value = dot(high, a_high, dims) + dot(low, a_high, dims) + dot(high, a_low, dims)
            copy.wait()
            return value

        if pairs:
            turned[...] = total[...].T

            @pl.when(valid)
            def _():
                turned[...] += part().T

            halve(turned, place_ref, keep, give, pairs)
        else:
            out[...] = total[...] if step else jnp.zeros_like(out)

            @pl.when(valid)
            def _():
                out[...] += part()

    halves = shape(matrix.shape[0], 2 * PANEL, dtype=BF16)
    if pairs:
        outs = (shape(width // 2, PANEL),) * 2 + (halves,)
    else:
        outs = (shape(PANEL, width), halves)
    return pl.pallas_call(
        body,
        in_specs=[SMEM, VMEM, VMEM] + ([VMEM, ANY] if step else []),
        out_specs=(VMEM,) * (len(outs) - 1) + (ANY,),
        out_shape=outs,
        input_output_aliases={4: len(outs) - 1} if step else {},
        scratch_shapes=[pltpu.VMEM((rows, 2 * PANEL), BF16), pltpu.SemaphoreType.DMA(())]
        + ([pltpu.VMEM((width, PANEL), F32)] if pairs else []),
        compiler_params=params(16),
        cost_estimate=small(),
        name="consume",
    )(place, matrix, sent, *before)


def solve(place, parts, hops):
    n, rows = len(parts), parts[0].shape[0]

    def body(col_ref, *refs):
        sources, (top, coeffs, inverse) = refs[n : n + len(hops)], refs[n + len(hops) :]
        for h, source in enumerate(sources):

            @pl.when(col_ref[0] == h)
            def _():
                inverse[...] = source[...]

        total = refs[0][...]
        for ref in refs[1:n]:
            total += ref[...]
        value = dot(total, inverse[...], ((1,), (1,)), HIGHEST)
        top[...] = value
        coeffs[...] = dot(value, inverse[...], ((1,), (0,)), HIGHEST)

    return pl.pallas_call(
        body,
        in_specs=[SMEM] + [VMEM] * (n + len(hops)),
        out_specs=(VMEM, VMEM),
        out_shape=(shape(rows, PANEL),) * 2,
        scratch_shapes=[pltpu.VMEM((PANEL, PANEL), F32)],
        compiler_params=params(4),
        cost_estimate=small(),
        name="solve",
    )(place, *parts, *hops)


def subtract(matrix, halves, coeffs):
    rows, width = matrix.shape
    tiles = 12
    size = rows // tiles
    slots = 3

    def body(a, p, c, out, ct, held, sems):
        ct_high, ct_low = split(c[...].T)
        ct[:PANEL, :] = ct_high
        ct[PANEL : 2 * PANEL, :] = ct_high
        ct[2 * PANEL :, :] = ct_low
        copies = [
            pltpu.make_async_copy(
                held.at[t % slots], out.at[pl.ds(t * size, size), :], sems.at[t % slots]
            )
            for t in range(tiles)
        ]
        for t in range(tiles):
            here = slice(t * size, (t + 1) * size)
            both = p[here, :]
            thrice = jnp.concatenate([both, both[:, :PANEL]], axis=1)
            value = a[here, :] - dot(thrice, ct[...], ((1,), (0,)))
            if t >= slots:
                copies[t - slots].wait()
            held[t % slots] = value
            copies[t].start()
        for t in range(tiles - slots, tiles):
            copies[t].wait()

    return pl.pallas_call(
        body,
        in_specs=[VMEM] * 3,
        out_specs=ANY,
        out_shape=shape(rows, width),
        scratch_shapes=[
            pltpu.VMEM((3 * PANEL, width), BF16),
            pltpu.VMEM((slots, size, width), F32),
            pltpu.SemaphoreType.DMA((slots,)),
        ],
        compiler_params=params(20),
        cost_estimate=small(),
        name="subtract",
    )(matrix, halves, coeffs)


def program(n_row, n_col):
    shift = [(h, h + 1) for h in range(n_col - 1)]
    pairs = n_row // 2

    def scatter(place, keep, give):
        got = lax.ppermute(give, "row", [(r, r ^ 1) for r in range(n_row)])
        parts = spread(place, keep, got, pairs)
        return [parts[0]] + [
            lax.ppermute(parts[j], "row", [(r, r ^ (2 * j)) for r in range(n_row)])
            for j in range(1, pairs)
        ]

    def shards(matrix):
        place = jnp.stack([lax.axis_index("col"), lax.axis_index("row")]).astype(jnp.int32)
        blocks = PANEL // BLOCK
        shifts = CHUNKS + 1 + LAG * (n_col - 2)
        last = CHUNKS - 1 + LAG * (n_col - 1)
        own = pack(matrix)
        sent, received, sums = [], [], []
        state = None
        done = 0
        for s in range(max(shifts, last + 1) + 1):
            if s < LAG:
                sent.append(own[s])
            elif s < shifts:
                after = [sums[s - LAG][0]] if s - LAG < len(sums) else []
                if state is not None:
                    after.append(state)
                source = own[s] if s < CHUNKS else state if s == CHUNKS else None
                x = received[s - LAG]
                sent.append(gate(x, *after) if source is None else fill(place, x, source, *after))
            elif s - LAG < shifts:
                sent.append(received[s - LAG])
            if s < shifts:
                received.append(lax.ppermute(sent[s], "col", shift))
            if s <= last:
                sums.append(
                    consume(
                        place,
                        matrix,
                        sent[s],
                        s,
                        sums[-1] if s else (),
                        pairs if s == last else 0,
                    )
                )
            if s == LAG - 1:
                state = add(scatter(place, *gram_part(place, own, pairs)))
            elif s == 2 * LAG - 1:
                state = lax.all_gather(gate(state, received[s - LAG]), "row", axis=0, tiled=True)
            elif s >= 2 * LAG and done < blocks:
                state = eliminate(place, gate(state, received[s - LAG]), done)
                done += 1
        keep, give, halves = sums[-1]
        parts = scatter(place, keep, give)
        top_rows, coeffs = solve(place, parts, [sent[CHUNKS + LAG * h] for h in range(n_col)])
        coeffs = lax.all_gather(coeffs, "row", axis=0, tiled=True)
        return top_rows, subtract(matrix, halves, coeffs)

    return shards


def solution(mesh):
    return jax.shard_map(
        program(mesh.shape["row"], mesh.shape["col"]),
        mesh=mesh,
        in_specs=(P("row", "col"),),
        out_specs=(P(("col", "row"), None), P("row", "col")),
        check_vma=False,
    )
```

```python
import jax
import jax.numpy as jnp
from jax import lax
from jax.experimental import pallas as pl
from jax.experimental.pallas import tpu as pltpu
from jax.sharding import PartitionSpec as P

PANEL = 256
CHUNKS = 16
LAG = 3
HALF = PANEL // 2
BLOCK = 32
HIGHEST = lax.Precision.HIGHEST
F32, BF16 = jnp.float32, jnp.bfloat16
ANY = pl.BlockSpec(memory_space=pl.ANY)
SMEM = pl.BlockSpec(memory_space=pltpu.SMEM)
VMEM = pl.BlockSpec(memory_space=pltpu.VMEM)


def params(mib):
    return pltpu.CompilerParams(vmem_limit_bytes=mib * 1024 * 1024)


def small():
    return pl.CostEstimate(flops=1, bytes_accessed=1, transcendentals=0)


def shape(*dims, dtype=F32):
    return jax.ShapeDtypeStruct(dims, dtype)


def split(x):
    hi = x.astype(BF16)
    return hi, (x - hi.astype(F32)).astype(BF16)


def dot(a, b, dims, precision=None):
    return lax.dot_general(
        a, b, (dims, ((), ())), precision=precision, preferred_element_type=F32
    )


def pack(col, row, matrix):
    rows = matrix.shape[0] // CHUNKS

    def body(col_ref, row_ref, source, *refs):
        outs, sems = refs[:LAG], refs[LAG]
        copies = [
            pltpu.make_async_copy(
                source.at[pl.ds(k * rows, rows), pl.ds(0, PANEL)], out, sems.at[k]
            )
            for k, out in enumerate(outs)
        ]
        for copy in copies:
            copy.start()
        for copy in copies:
            copy.wait()

    return pl.pallas_call(
        body,
        in_specs=[SMEM, SMEM, ANY],
        out_specs=(VMEM,) * LAG,
        out_shape=(shape(rows, PANEL),) * LAG,
        scratch_shapes=[pltpu.SemaphoreType.DMA((LAG,))],
        compiler_params=params(8),
        cost_estimate=small(),
        name="pack",
    )(col, row, matrix)


def gate(x, *after):
    def body(*refs):
        pass

    return pl.pallas_call(
        body,
        in_specs=[ANY] * (1 + len(after)),
        out_specs=ANY,
        out_shape=shape(*x.shape, dtype=x.dtype),
        input_output_aliases={0: 0},
        compiler_params=params(1),
        cost_estimate=small(),
        name="gate",
    )(x, *after)


def fill(col, received, source, chunk, *after):
    rows = received.shape[0]

    def body(col_ref, _, source_ref, *refs):
        out, sem = refs[-2:]

        @pl.when(col_ref[0] == 0)
        def _():
            if chunk is None:
                copy = pltpu.make_async_copy(source_ref, out.at[pl.ds(0, source.shape[0]), :], sem)
            else:
                own = source_ref.at[pl.ds(chunk * rows, rows), pl.ds(0, PANEL)]
                copy = pltpu.make_async_copy(own, out, sem)
            copy.start()
            copy.wait()

    return pl.pallas_call(
        body,
        in_specs=[SMEM] + [ANY] * (2 + len(after)),
        out_specs=ANY,
        out_shape=shape(*received.shape),
        input_output_aliases={1: 0},
        scratch_shapes=[pltpu.SemaphoreType.DMA(())],
        compiler_params=params(1),
        cost_estimate=small(),
        name="fill",
    )(col, received, source, *after)


def halve(total, row_ref, keep, give, pairs):
    size = total.shape[0] // (2 * pairs)
    core = row_ref[0] % 2
    for k in range(pairs):
        here = slice(k * size, (k + 1) * size)
        mine = pl.multiple_of((2 * k + core) * size, size)
        other = pl.multiple_of((2 * k + 1 - core) * size, size)
        keep[here, :] = total[pl.ds(mine, size), :]
        give[here, :] = total[pl.ds(other, size), :]


def spread(row, keep, got, pairs):
    size = keep.shape[0] // pairs

    def body(row_ref, keep_ref, got_ref, *outs):
        chip = row_ref[0] // 2
        for j, out in enumerate(outs):
            here = pl.ds(pl.multiple_of((chip ^ j) * size, size), size)
            out[...] = keep_ref[here, :] + got_ref[here, :]

    return pl.pallas_call(
        body,
        in_specs=[SMEM, VMEM, VMEM],
        out_specs=(VMEM,) * pairs,
        out_shape=(shape(size, PANEL),) * pairs,
        compiler_params=params(4),
        cost_estimate=small(),
        name="spread",
    )(row, keep, got)


def add(parts):
    def body(*refs):
        total = refs[0][...]
        for ref in refs[1:-1]:
            total += ref[...]
        refs[-1][...] = total

    return pl.pallas_call(
        body,
        in_specs=[VMEM] * len(parts),
        out_specs=VMEM,
        out_shape=shape(*parts[0].shape),
        compiler_params=params(2),
        cost_estimate=small(),
        name="add",
    )(*parts)


def gram_part(col, row, matrix):
    tiles = 4
    rows = matrix.shape[0] // tiles

    def body(col_ref, row_ref, source, keep, give, held, sems):
        @pl.when(col_ref[0] == 0)
        def _():
            copies = [
                pltpu.make_async_copy(
                    source.at[pl.ds(t * rows, rows), pl.ds(0, PANEL)], held.at[t], sems.at[t]
                )
                for t in range(tiles)
            ]
            for copy in copies:
                copy.start()
            square = jnp.zeros((PANEL, PANEL), F32)
            cross = jnp.zeros((PANEL, PANEL), F32)
            dims = ((0,), (0,))
            for t in range(tiles):
                copies[t].wait()
                high, low = split(held[t])
                square += dot(high, high, dims) + dot(low, low, dims)
                cross += dot(high, low, dims)
            total = square + (cross + cross.T)
            upper = row_ref[0] % 2 == 0
            keep[...] = jnp.where(upper, total[:HALF, :], total[HALF:, :])
            give[...] = jnp.where(upper, total[HALF:, :], total[:HALF, :])

    return pl.pallas_call(
        body,
        in_specs=[SMEM, SMEM, ANY],
        out_specs=(VMEM, VMEM),
        out_shape=(shape(HALF, PANEL),) * 2,
        scratch_shapes=[
            pltpu.VMEM((tiles, rows, PANEL), F32),
            pltpu.SemaphoreType.DMA((tiles,)),
        ],
        compiler_params=params(12),
        cost_estimate=small(),
        name="gram",
    )(col, row, matrix)


def eliminate(col, row, state, block):
    first, last = block * BLOCK, (block + 1) * BLOCK
    width = 2 * PANEL

    def body(col_ref, row_ref, src, *rest):
        out, packed = (rest[-2:] if last == PANEL else (rest[-1], None))

        @pl.when(col_ref[0] == 0)
        def _():
            if block == 0:
                row = lax.broadcasted_iota(jnp.int32, (PANEL, PANEL), 0)
                lane = lax.broadcasted_iota(jnp.int32, (PANEL, PANEL), 1)
                upper = row_ref[0] % 2 == 0
                out[:HALF, :PANEL] = jnp.where(upper, src[...], rest[0][...])
                out[HALF:, :PANEL] = jnp.where(upper, rest[0][...], src[...])
                out[:, PANEL:] = (row == lane).astype(F32)
            else:
                out[...] = src[...]
            row = lax.broadcasted_iota(jnp.int32, (BLOCK, BLOCK), 0)
            lane = lax.broadcasted_iota(jnp.int32, (BLOCK, BLOCK), 1)
            work = jnp.concatenate(
                [out[first:last, first:last], (row == lane).astype(F32)], axis=1
            )
            below = lax.broadcasted_iota(jnp.int32, (BLOCK, 2 * BLOCK), 0)
            scale = jnp.zeros((BLOCK, 2 * BLOCK), F32)
            for i in range(0, BLOCK, 2):
                column = jnp.broadcast_to(work[:, i : i + 1], work.shape)
                follow = jnp.broadcast_to(work[:, i + 1 : i + 2], work.shape)
                upper, lower = work[i : i + 1, :], work[i + 1 : i + 2, :]
                pivot, cross = column[i : i + 1, :], column[i + 1 : i + 2, :]
                inverse = 1.0 / pivot
                ratio = cross * inverse
                second = follow[i + 1 : i + 2, :] - ratio * follow[i : i + 1, :]
                factor = jnp.where(below > i, column * inverse, 0.0)
                follow = follow - factor * follow[i : i + 1, :]
                after = jnp.where(below > i + 1, follow * (1.0 / second), 0.0)
                lower = lower - ratio * upper
                work = work - factor * upper - after * lower
                scale = jnp.where(below == i, pivot, jnp.where(below == i + 1, second, scale))
            root = lax.rsqrt(scale)
            root = root * (1.5 - 0.5 * scale * root * root)
            rows = dot((work * root)[:, BLOCK:], out[first:last, :], ((1,), (0,)), HIGHEST)
            out[first:last, :] = rows
            if last == PANEL:
                packed[:HALF, :] = out[HALF:, PANEL:]
                packed[HALF:, :HALF] = out[: HALF // 2, PANEL : PANEL + HALF]
                packed[HALF:, HALF:] = out[HALF // 2 : HALF, PANEL : PANEL + HALF]
            else:
                left, right = last // 128 * 128, PANEL + -(-last // 128) * 128
                out[last:, left:right] -= dot(
                    rows[:, last:PANEL], rows[:, left:right], ((0,), (0,)), HIGHEST
                )

    return pl.pallas_call(
        body,
        in_specs=[SMEM, SMEM] + [VMEM] * len(state),
        out_specs=(VMEM, VMEM) if last == PANEL else VMEM,
        out_shape=(shape(PANEL, width), shape(HALF + HALF // 2, PANEL))
        if last == PANEL
        else shape(PANEL, width),
        input_output_aliases={2: 0} if block else {},
        compiler_params=params(8),
        cost_estimate=small(),
        name=f"eliminate{block}",
    )(col, row, *state)


def consume(col, row, matrix, sent, step, before, pairs):
    rows, width = sent.shape[0], matrix.shape[1]

    def body(col_ref, row_ref, block, source, *refs):
        if pairs:
            total, _, keep, give, halves, held, sem, turned = refs
        elif step > LAG:
            total, _, out, halves, held, sem = refs
        else:
            out, halves, held, sem = refs
        chunk = step - LAG * col_ref[0]

        def part(chunk, piece):
            here = pl.ds(pl.multiple_of(chunk * rows, rows), rows)
            high, low = split(piece)
            held[:, :PANEL] = high
            held[:, PANEL:] = low
            copy = pltpu.make_async_copy(held, halves.at[here, :], sem)
            copy.start()
            a_high, a_low = split(block[here, :])
            dims = ((0,), (0,))
            value = dot(high, a_high, dims) + dot(low, a_high, dims) + dot(high, a_low, dims)
            copy.wait()
            return value

        valid = (col_ref[0] > 0) & (chunk >= 0) & (chunk < CHUNKS)
        if pairs:
            turned[...] = total[...].T

            @pl.when(valid)
            def _():
                turned[...] += part(chunk, source[...]).T

            halve(turned, row_ref, keep, give, pairs)
        else:
            out[...] = total[...] if step > LAG else jnp.zeros_like(out)

            @pl.when(valid)
            def _():
                out[...] += part(chunk, source[...])

            if step == CHUNKS + 1:

                @pl.when(col_ref[0] == 0)
                def _():
                    @pl.loop(0, CHUNKS)
                    def _(k):
                        here = pl.ds(pl.multiple_of(k * rows, rows), rows)
                        out[...] += part(k, block[here, :PANEL])

    halves = shape(matrix.shape[0], 2 * PANEL, dtype=BF16)
    if pairs:
        outs = (shape(width // 2, PANEL),) * 2 + (halves,)
    else:
        outs = (shape(PANEL, width), halves)
    return pl.pallas_call(
        body,
        in_specs=[SMEM, SMEM, VMEM, VMEM] + ([VMEM, ANY] if step > LAG else []),
        out_specs=(VMEM,) * (len(outs) - 1) + (ANY,),
        out_shape=outs,
        input_output_aliases={5: len(outs) - 1} if step > LAG else {},
        scratch_shapes=[pltpu.VMEM((rows, 2 * PANEL), BF16), pltpu.SemaphoreType.DMA(())]
        + ([pltpu.VMEM((width, PANEL), F32)] if pairs else []),
        compiler_params=params(16),
        cost_estimate=small(),
        name="consume",
    )(col, row, matrix, sent, *before)


def solve(col, parts, hops):
    n, rows = len(parts), parts[0].shape[0]

    def body(col_ref, *refs):
        sources, (top, coeffs, inverse) = refs[n : n + len(hops)], refs[n + len(hops) :]
        for h, source in enumerate(sources):

            @pl.when(col_ref[0] == h)
            def _():
                inverse[HALF:, :] = source[:HALF, :]
                inverse[: HALF // 2, :HALF] = source[HALF : HALF + HALF // 2, :HALF]
                inverse[HALF // 2 : HALF, :HALF] = source[HALF : HALF + HALF // 2, HALF:]
                inverse[:HALF, HALF:] = jnp.zeros((HALF, HALF), F32)

        total = refs[0][...]
        for ref in refs[1:n]:
            total += ref[...]
        value = dot(total, inverse[...], ((1,), (1,)), HIGHEST)
        top[...] = value
        coeffs[...] = dot(value, inverse[...], ((1,), (0,)), HIGHEST)

    return pl.pallas_call(
        body,
        in_specs=[SMEM] + [VMEM] * (n + len(hops)),
        out_specs=(VMEM, VMEM),
        out_shape=(shape(rows, PANEL),) * 2,
        scratch_shapes=[pltpu.VMEM((PANEL, PANEL), F32)],
        compiler_params=params(4),
        cost_estimate=small(),
        name="solve",
    )(col, *parts, *hops)


def subtract(matrix, halves, coeffs):
    rows, width = matrix.shape
    tiles = 12
    size = rows // tiles
    slots = 3

    def body(a, p, c, out, ct, held, sems):
        ct_high, ct_low = split(c[...].T)
        ct[:PANEL, :] = ct_high
        ct[PANEL : 2 * PANEL, :] = ct_high
        ct[2 * PANEL :, :] = ct_low
        copies = [
            pltpu.make_async_copy(
                held.at[t % slots], out.at[pl.ds(t * size, size), :], sems.at[t % slots]
            )
            for t in range(tiles)
        ]
        for t in range(tiles):
            here = slice(t * size, (t + 1) * size)
            both = p[here, :]
            thrice = jnp.concatenate([both, both[:, :PANEL]], axis=1)
            value = a[here, :] - dot(thrice, ct[...], ((1,), (0,)))
            if t >= slots:
                copies[t - slots].wait()
            held[t % slots] = value
            copies[t].start()
        for t in range(tiles - slots, tiles):
            copies[t].wait()

    return pl.pallas_call(
        body,
        in_specs=[VMEM] * 3,
        out_specs=ANY,
        out_shape=shape(rows, width),
        scratch_shapes=[
            pltpu.VMEM((3 * PANEL, width), BF16),
            pltpu.VMEM((slots, size, width), F32),
            pltpu.SemaphoreType.DMA((slots,)),
        ],
        compiler_params=params(20),
        cost_estimate=small(),
        name="subtract",
    )(matrix, halves, coeffs)


def program(n_row, n_col):
    pairs = n_row // 2

    def swap(x, bit):
        return lax.ppermute(x, "row", [(r, r ^ bit) for r in range(n_row)])

    def scatter(row, keep, give):
        parts = spread(row, keep, swap(give, 1), pairs)
        return [parts[0]] + [swap(parts[j], 2 * j) for j in range(1, pairs)]

    def shards(matrix):
        col = lax.axis_index("col").astype(jnp.int32).reshape(1)
        row = lax.axis_index("row").astype(jnp.int32).reshape(1)
        blocks = PANEL // BLOCK
        shifts = CHUNKS + 1 + LAG * (n_col - 2)
        last = CHUNKS - 1 + LAG * (n_col - 1)
        own = pack(col, row, matrix)
        keep, give = gram_part(col, row, matrix)
        half = add([keep, swap(give, 1)])
        sent, received, sums = [], [], {}
        state = packed = None
        done = 0
        for s in range(max(shifts, last + 1) + 1):
            if s < LAG:
                sent.append(own[s])
            elif s < shifts:
                after = [sums[s - 2 * LAG][0]] if s - 2 * LAG in sums else []
                if s == LAG:
                    after.append(half)
                elif state is not None:
                    after.append(state[0])
                x = received[s - LAG]
                if s < CHUNKS:
                    sent.append(fill(col, x, matrix, s, *after))
                elif s == CHUNKS:
                    sent.append(fill(col, x, packed, None, *after))
                else:
                    sent.append(gate(x, *after))
            elif s - LAG < shifts:
                sent.append(received[s - LAG])
            if s < shifts:
                hops = [(h, h + 1) for h in range(n_col - 1) if 0 <= s - LAG * h <= CHUNKS]
                received.append(lax.ppermute(sent[s], "col", hops))
            if LAG <= s <= last:
                before = sums[s - 1] if s > LAG else ()
                sums[s] = consume(
                    col, row, matrix, sent[s], s, before, pairs if s == last else 0
                )
            if s == LAG:
                state = [add([half] + [swap(half, 2 * j) for j in range(1, pairs)])]
            elif s == LAG + 1:
                mine = gate(state[0], sent[s])
                state = [mine, swap(mine, 1)]
            elif s > LAG + 1 and done < blocks and (s - LAG) % 4:
                state = eliminate(col, row, [gate(state[0], sent[s]), *state[1:]], done)
                done += 1
                state = [state] if done < blocks else state
                if done == blocks:
                    packed = state[1]
        keep, give, halves = sums[last]
        parts = scatter(row, keep, give)
        top_rows, coeffs = solve(col, parts, [sent[CHUNKS + LAG * h] for h in range(n_col)])
        coeffs = lax.all_gather(coeffs, "row", axis=0, tiled=True)
        return top_rows, subtract(matrix, halves, coeffs)

    return shards


def solution(mesh):
    return jax.shard_map(
        program(mesh.shape["row"], mesh.shape["col"]),
        mesh=mesh,
        in_specs=(P("row", "col"),),
        out_specs=(P(("col", "row"), None), P("row", "col")),
        check_vma=False,
    )
```

```python
import jax
import jax.numpy as jnp
from jax import lax
from jax.experimental import pallas as pl
from jax.experimental.pallas import tpu as pltpu
from jax.sharding import PartitionSpec as P

PANEL = 256
CHUNKS = 16
LAG = 3
HALF = PANEL // 2
BLOCK = 32
HIGHEST = lax.Precision.HIGHEST
F32, BF16 = jnp.float32, jnp.bfloat16
ANY = pl.BlockSpec(memory_space=pl.ANY)
SMEM = pl.BlockSpec(memory_space=pltpu.SMEM)
VMEM = pl.BlockSpec(memory_space=pltpu.VMEM)


def params(mib):
    return pltpu.CompilerParams(vmem_limit_bytes=mib * 1024 * 1024)


def small():
    return pl.CostEstimate(flops=1, bytes_accessed=1, transcendentals=0)


def shape(*dims, dtype=F32):
    return jax.ShapeDtypeStruct(dims, dtype)


def split(x):
    hi = x.astype(BF16)
    return hi, (x - hi.astype(F32)).astype(BF16)


def dot(a, b, dims, precision=None):
    return lax.dot_general(
        a, b, (dims, ((), ())), precision=precision, preferred_element_type=F32
    )


def gate(x, *after):
    def body(*refs):
        pass

    return pl.pallas_call(
        body,
        in_specs=[ANY] * (1 + len(after)),
        out_specs=ANY,
        out_shape=shape(*x.shape, dtype=x.dtype),
        input_output_aliases={0: 0},
        compiler_params=params(1),
        cost_estimate=small(),
        name="gate",
    )(x, *after)


def fill(col, received, source, first, *after):
    rows = min(received.shape[0], source.shape[0] - first)

    def body(col_ref, _, source_ref, *refs):
        out, sem = refs[-2:]

        @pl.when(col_ref[0] == 0)
        def _():
            own = source_ref.at[pl.ds(first, rows), pl.ds(0, PANEL)]
            copy = pltpu.make_async_copy(own, out.at[pl.ds(0, rows), :], sem)
            copy.start()
            copy.wait()

    return pl.pallas_call(
        body,
        in_specs=[SMEM] + [ANY] * (2 + len(after)),
        out_specs=ANY,
        out_shape=shape(*received.shape),
        input_output_aliases={1: 0},
        scratch_shapes=[pltpu.SemaphoreType.DMA(())],
        compiler_params=params(1),
        cost_estimate=small(),
        name="fill",
    )(col, received, source, *after)


def halve(total, row_ref, keep, give, pairs):
    size = total.shape[0] // (2 * pairs)
    core = row_ref[0] % 2
    for k in range(pairs):
        here = slice(k * size, (k + 1) * size)
        mine = pl.multiple_of((2 * k + core) * size, size)
        other = pl.multiple_of((2 * k + 1 - core) * size, size)
        keep[here, :] = total[pl.ds(mine, size), :]
        give[here, :] = total[pl.ds(other, size), :]


def spread(row, keep, got, pairs):
    size = keep.shape[0] // pairs

    def body(row_ref, keep_ref, got_ref, *outs):
        chip = row_ref[0] // 2
        for j, out in enumerate(outs):
            here = pl.ds(pl.multiple_of((chip ^ j) * size, size), size)
            out[...] = keep_ref[here, :] + got_ref[here, :]

    return pl.pallas_call(
        body,
        in_specs=[SMEM, VMEM, VMEM],
        out_specs=(VMEM,) * pairs,
        out_shape=(shape(size, PANEL),) * pairs,
        compiler_params=params(4),
        cost_estimate=small(),
        name="spread",
    )(row, keep, got)


def add(parts):
    def body(*refs):
        total = refs[0][...]
        for ref in refs[1:-1]:
            total += ref[...]
        refs[-1][...] = total

    return pl.pallas_call(
        body,
        in_specs=[VMEM] * len(parts),
        out_specs=VMEM,
        out_shape=shape(*parts[0].shape),
        compiler_params=params(2),
        cost_estimate=small(),
        name="add",
    )(*parts)


def gram_part(col, row, matrix):
    tiles = 8
    rows = matrix.shape[0] // tiles

    def body(col_ref, row_ref, source, keep, give, held, sems):
        @pl.when(col_ref[0] == 0)
        def _():
            copies = [
                pltpu.make_async_copy(
                    source.at[pl.ds(t * rows, rows), pl.ds(0, PANEL)], held.at[t], sems.at[t]
                )
                for t in range(tiles)
            ]
            for copy in copies:
                copy.start()
            square = jnp.zeros((PANEL, PANEL), F32)
            cross = jnp.zeros((PANEL, PANEL), F32)
            dims = ((0,), (0,))
            for t in range(tiles):
                copies[t].wait()
                high, low = split(held[t])
                square += dot(high, high, dims) + dot(low, low, dims)
                cross += dot(high, low, dims)
            total = square + (cross + cross.T)
            upper = row_ref[0] % 2 == 0
            keep[...] = jnp.where(upper, total[:HALF, :], total[HALF:, :])
            give[...] = jnp.where(upper, total[HALF:, :], total[:HALF, :])

    return pl.pallas_call(
        body,
        in_specs=[SMEM, SMEM, ANY],
        out_specs=(VMEM, VMEM),
        out_shape=(shape(HALF, PANEL),) * 2,
        scratch_shapes=[
            pltpu.VMEM((tiles, rows, PANEL), F32),
            pltpu.SemaphoreType.DMA((tiles,)),
        ],
        compiler_params=params(55),
        cost_estimate=small(),
        name="gram",
    )(col, row, matrix)


def eliminate(col, row, state, block):
    first, last = block * BLOCK, (block + 1) * BLOCK
    width = 2 * PANEL

    def body(col_ref, row_ref, src, *rest):
        out, packed = (rest[-2:] if last == PANEL else (rest[-1], None))

        @pl.when(col_ref[0] == 0)
        def _():
            if block == 0:
                row = lax.broadcasted_iota(jnp.int32, (PANEL, PANEL), 0)
                lane = lax.broadcasted_iota(jnp.int32, (PANEL, PANEL), 1)
                upper = row_ref[0] % 2 == 0
                out[:HALF, :PANEL] = jnp.where(upper, src[...], rest[0][...])
                out[HALF:, :PANEL] = jnp.where(upper, rest[0][...], src[...])
                out[:, PANEL:] = (row == lane).astype(F32)
            else:
                out[...] = src[...]
            row = lax.broadcasted_iota(jnp.int32, (BLOCK, BLOCK), 0)
            lane = lax.broadcasted_iota(jnp.int32, (BLOCK, BLOCK), 1)
            work = jnp.concatenate(
                [out[first:last, first:last], (row == lane).astype(F32)], axis=1
            )
            below = lax.broadcasted_iota(jnp.int32, (BLOCK, 2 * BLOCK), 0)
            scale = jnp.zeros((BLOCK, 2 * BLOCK), F32)
            for i in range(0, BLOCK, 2):
                column = jnp.broadcast_to(work[:, i : i + 1], work.shape)
                follow = jnp.broadcast_to(work[:, i + 1 : i + 2], work.shape)
                upper, lower = work[i : i + 1, :], work[i + 1 : i + 2, :]
                pivot, cross = column[i : i + 1, :], column[i + 1 : i + 2, :]
                inverse = 1.0 / pivot
                ratio = cross * inverse
                second = follow[i + 1 : i + 2, :] - ratio * follow[i : i + 1, :]
                factor = jnp.where(below > i, column * inverse, 0.0)
                follow = follow - factor * follow[i : i + 1, :]
                after = jnp.where(below > i + 1, follow * (1.0 / second), 0.0)
                lower = lower - ratio * upper
                work = work - factor * upper - after * lower
                scale = jnp.where(below == i, pivot, jnp.where(below == i + 1, second, scale))
            root = lax.rsqrt(scale)
            root = root * (1.5 - 0.5 * scale * root * root)
            rows = dot((work * root)[:, BLOCK:], out[first:last, :], ((1,), (0,)), HIGHEST)
            out[first:last, :] = rows
            if last == PANEL:
                packed[:HALF, :] = out[HALF:, PANEL:]
                packed[HALF:, :HALF] = out[: HALF // 2, PANEL : PANEL + HALF]
                packed[HALF:, HALF:] = out[HALF // 2 : HALF, PANEL : PANEL + HALF]
            else:
                left, right = last // 128 * 128, PANEL + -(-last // 128) * 128
                out[last:, left:right] -= dot(
                    rows[:, last:PANEL], rows[:, left:right], ((0,), (0,)), HIGHEST
                )

    return pl.pallas_call(
        body,
        in_specs=[SMEM, SMEM] + [VMEM] * len(state),
        out_specs=(VMEM, VMEM) if last == PANEL else VMEM,
        out_shape=(shape(PANEL, width), shape(HALF + HALF // 2, PANEL))
        if last == PANEL
        else shape(PANEL, width),
        input_output_aliases={2: 0} if block else {},
        compiler_params=params(8),
        cost_estimate=small(),
        name=f"eliminate{block}",
    )(col, row, *state)


def consume(col, row, matrix, sent, step, before, pairs):
    rows, width = sent.shape[0], matrix.shape[1]

    def body(col_ref, row_ref, block, source, *refs):
        if pairs:
            total, _, keep, give, halves, held, sem, turned = refs
        elif step > LAG:
            total, _, out, halves, held, sem = refs
        else:
            out, halves, held, sem = refs
        chunk = step - LAG * col_ref[0]

        def part(chunk, piece):
            here = pl.ds(pl.multiple_of(chunk * rows, rows), rows)
            high, low = split(piece)
            held[:, :PANEL] = high
            held[:, PANEL:] = low
            copy = pltpu.make_async_copy(held, halves.at[here, :], sem)
            copy.start()
            a_high, a_low = split(block[here, :])
            dims = ((0,), (0,))
            value = dot(high, a_high, dims) + dot(low, a_high, dims) + dot(high, a_low, dims)
            copy.wait()
            return value

        valid = (col_ref[0] > 0) & (chunk >= 0) & (chunk < CHUNKS)
        if pairs:
            turned[...] = total[...].T

            @pl.when(valid)
            def _():
                turned[...] += part(chunk, source[...]).T

            halve(turned, row_ref, keep, give, pairs)
        else:
            out[...] = total[...] if step > LAG else jnp.zeros_like(out)

            @pl.when(valid)
            def _():
                out[...] += part(chunk, source[...])

            if step == CHUNKS + 1:

                @pl.when(col_ref[0] == 0)
                def _():
                    @pl.loop(0, CHUNKS)
                    def _(k):
                        here = pl.ds(pl.multiple_of(k * rows, rows), rows)
                        out[...] += part(k, block[here, :PANEL])

    halves = shape(matrix.shape[0], 2 * PANEL, dtype=BF16)
    if pairs:
        outs = (shape(width // 2, PANEL),) * 2 + (halves,)
    else:
        outs = (shape(PANEL, width), halves)
    return pl.pallas_call(
        body,
        in_specs=[SMEM, SMEM, VMEM, VMEM] + ([VMEM, ANY] if step > LAG else []),
        out_specs=(VMEM,) * (len(outs) - 1) + (ANY,),
        out_shape=outs,
        input_output_aliases={5: len(outs) - 1} if step > LAG else {},
        scratch_shapes=[pltpu.VMEM((rows, 2 * PANEL), BF16), pltpu.SemaphoreType.DMA(())]
        + ([pltpu.VMEM((width, PANEL), F32)] if pairs else []),
        compiler_params=params(16),
        cost_estimate=small(),
        name="consume",
    )(col, row, matrix, sent, *before)


def solve(col, parts, hops):
    n, rows = len(parts), parts[0].shape[0]
    pieces, size = len(hops[0]), hops[0][0].shape[0]

    def body(col_ref, *refs):
        sources, (top, coeffs, inverse, packed) = refs[n:-4], refs[-4:]
        for h in range(len(hops)):

            @pl.when(col_ref[0] == h)
            def _():
                for p in range(pieces):
                    packed[p * size : (p + 1) * size, :] = sources[h * pieces + p][...]

        inverse[HALF:, :] = packed[:HALF, :]
        inverse[: HALF // 2, :HALF] = packed[HALF : HALF + HALF // 2, :HALF]
        inverse[HALF // 2 : HALF, :HALF] = packed[HALF : HALF + HALF // 2, HALF:]
        inverse[:HALF, HALF:] = jnp.zeros((HALF, HALF), F32)
        total = refs[0][...]
        for ref in refs[1:n]:
            total += ref[...]
        value = dot(total, inverse[...], ((1,), (1,)), HIGHEST)
        top[...] = value
        coeffs[...] = dot(value, inverse[...], ((1,), (0,)), HIGHEST)

    return pl.pallas_call(
        body,
        in_specs=[SMEM] + [VMEM] * (n + len(hops) * pieces),
        out_specs=(VMEM, VMEM),
        out_shape=(shape(rows, PANEL),) * 2,
        scratch_shapes=[pltpu.VMEM((PANEL, PANEL), F32), pltpu.VMEM((pieces * size, PANEL), F32)],
        compiler_params=params(6),
        cost_estimate=small(),
        name="solve",
    )(col, *parts, *[piece for hop in hops for piece in hop])


def subtract(matrix, halves, coeffs):
    rows, width = matrix.shape
    tiles = 12
    size = rows // tiles

    def body(a, p, c, out, ct, held, sems):
        ct_high, ct_low = split(c[...].T)
        ct[:PANEL, :] = ct_high
        ct[PANEL : 2 * PANEL, :] = ct_high
        ct[2 * PANEL :, :] = ct_low
        copies = [
            pltpu.make_async_copy(held.at[t], out.at[pl.ds(t * size, size), :], sems.at[t])
            for t in range(tiles)
        ]
        for t in range(tiles):
            here = slice(t * size, (t + 1) * size)
            both = p[here, :]
            thrice = jnp.concatenate([both, both[:, :PANEL]], axis=1)
            value = a[here, :] - dot(thrice, ct[...], ((1,), (0,)))
            held[t] = value
            copies[t].start()
        for copy in copies:
            copy.wait()

    return pl.pallas_call(
        body,
        in_specs=[VMEM] * 3,
        out_specs=ANY,
        out_shape=shape(rows, width),
        scratch_shapes=[
            pltpu.VMEM((3 * PANEL, width), BF16),
            pltpu.VMEM((tiles, size, width), F32),
            pltpu.SemaphoreType.DMA((tiles,)),
        ],
        compiler_params=params(20),
        cost_estimate=small(),
        name="subtract",
    )(matrix, halves, coeffs)


def program(n_row, n_col):
    pairs = n_row // 2

    def swap(x, bit):
        return lax.ppermute(x, "row", [(r, r ^ bit) for r in range(n_row)])

    def scatter(row, keep, give):
        parts = spread(row, keep, swap(give, 1), pairs)
        return [parts[0]] + [swap(parts[j], 2 * j) for j in range(1, pairs)]

    def shards(matrix):
        col = lax.axis_index("col").astype(jnp.int32).reshape(1)
        row = lax.axis_index("row").astype(jnp.int32).reshape(1)
        blocks = PANEL // BLOCK
        rows = matrix.shape[0] // CHUNKS
        pieces = -(-(HALF + HALF // 2) // rows)
        shifts = CHUNKS + pieces + LAG * (n_col - 2)
        last = CHUNKS - 1 + LAG * (n_col - 1)
        first = LAG + 2
        due = [first + i * (CHUNKS - 1 - first) // (blocks - 1) for i in range(blocks)]
        sent, received, sums = [], [], {}
        half = state = packed = None
        for s in range(shifts + LAG):
            if s < LAG:
                sent.append(matrix[s * rows : (s + 1) * rows, :PANEL])
            elif s < shifts:
                after = [sums[s - 2 * LAG][0]] if s - 2 * LAG in sums else []
                if s == LAG:
                    keep, give = gram_part(col, row, matrix)
                    half = add([keep, swap(give, 1)])
                    after.append(half)
                elif state is not None:
                    after.append(state[0])
                x = received[s - LAG]
                if s < CHUNKS:
                    sent.append(fill(col, x, matrix, s * rows, *after))
                elif s < CHUNKS + pieces:
                    sent.append(fill(col, x, packed, (s - CHUNKS) * rows, *after))
                else:
                    sent.append(gate(x, *after))
            else:
                sent.append(received[s - LAG])
            if s < shifts:
                hops = [(h, h + 1) for h in range(n_col - 1) if 0 <= s - LAG * h < CHUNKS + pieces]
                received.append(lax.ppermute(sent[s], "col", hops))
            if LAG <= s <= last:
                before = sums[s - 1] if s > LAG else ()
                sums[s] = consume(
                    col, row, matrix, sent[s], s, before, pairs if s == last else 0
                )
            if s == LAG:
                state = [add([half] + [swap(half, 2 * j) for j in range(1, pairs)])]
            elif s == LAG + 1:
                mine = gate(state[0], sent[s])
                state = [mine, swap(mine, 1)]
            elif s in due:
                block = due.index(s)
                state = eliminate(col, row, [gate(state[0], sent[s]), *state[1:]], block)
                if block == blocks - 1:
                    state, packed = [state[0]], state[1]
                else:
                    state = [state]
        keep, give, halves = sums[last]
        parts = scatter(row, keep, give)
        inverse = [
            [sent[CHUNKS + p + LAG * h] for p in range(pieces)] for h in range(n_col)
        ]
        top_rows, coeffs = solve(col, parts, inverse)
        coeffs = lax.all_gather(coeffs, "row", axis=0, tiled=True)
        return top_rows, subtract(matrix, halves, coeffs)

    return shards


def solution(mesh):
    return jax.shard_map(
        program(mesh.shape["row"], mesh.shape["col"]),
        mesh=mesh,
        in_specs=(P("row", "col"),),
        out_specs=(P(("col", "row"), None), P("row", "col")),
        check_vma=False,
    )
```

```python
import jax
import jax.numpy as jnp
from jax import lax
from jax.experimental import pallas as pl
from jax.experimental.pallas import tpu as pltpu
from jax.sharding import PartitionSpec as P

PANEL = 256
CHUNKS = 16
LAG = 3
HALF = PANEL // 2
OWN = 4
BLOCK = 32
HIGHEST = lax.Precision.HIGHEST
F32, BF16 = jnp.float32, jnp.bfloat16
ANY = pl.BlockSpec(memory_space=pl.ANY)
SMEM = pl.BlockSpec(memory_space=pltpu.SMEM)
VMEM = pl.BlockSpec(memory_space=pltpu.VMEM)


def params(mib):
    return pltpu.CompilerParams(vmem_limit_bytes=mib * 1024 * 1024)


def small():
    return pl.CostEstimate(flops=1, bytes_accessed=1, transcendentals=0)


def shape(*dims, dtype=F32):
    return jax.ShapeDtypeStruct(dims, dtype)


def split(x):
    hi = x.astype(BF16)
    return hi, (x - hi.astype(F32)).astype(BF16)


def dot(a, b, dims, precision=None):
    return lax.dot_general(
        a, b, (dims, ((), ())), precision=precision, preferred_element_type=F32
    )


def gate(x, *after):
    def body(*refs):
        pass

    return pl.pallas_call(
        body,
        in_specs=[ANY] * (1 + len(after)),
        out_specs=ANY,
        out_shape=shape(*x.shape, dtype=x.dtype),
        input_output_aliases={0: 0},
        compiler_params=params(1),
        cost_estimate=small(),
        name="gate",
    )(x, *after)


def fill(col, received, source, first, *after):
    rows = min(received.shape[0], source.shape[0] - first)

    def body(col_ref, _, source_ref, *refs):
        out, sem = refs[-2:]

        @pl.when(col_ref[0] == 0)
        def _():
            own = source_ref.at[pl.ds(first, rows), pl.ds(0, PANEL)]
            copy = pltpu.make_async_copy(own, out.at[pl.ds(0, rows), :], sem)
            copy.start()
            copy.wait()

    return pl.pallas_call(
        body,
        in_specs=[SMEM] + [ANY] * (2 + len(after)),
        out_specs=ANY,
        out_shape=shape(*received.shape),
        input_output_aliases={1: 0},
        scratch_shapes=[pltpu.SemaphoreType.DMA(())],
        compiler_params=params(1),
        cost_estimate=small(),
        name="fill",
    )(col, received, source, *after)


def halve(total, row_ref, keep, give, pairs):
    size = total.shape[0] // (2 * pairs)
    core = row_ref[0] % 2
    for k in range(pairs):
        here = slice(k * size, (k + 1) * size)
        mine = pl.multiple_of((2 * k + core) * size, size)
        other = pl.multiple_of((2 * k + 1 - core) * size, size)
        keep[here, :] = total[pl.ds(mine, size), :]
        give[here, :] = total[pl.ds(other, size), :]


def spread(row, keep, got, pairs):
    size = keep.shape[0] // pairs

    def body(row_ref, keep_ref, got_ref, *outs):
        chip = row_ref[0] // 2
        for j, out in enumerate(outs):
            here = pl.ds(pl.multiple_of((chip ^ j) * size, size), size)
            out[...] = keep_ref[here, :] + got_ref[here, :]

    return pl.pallas_call(
        body,
        in_specs=[SMEM, VMEM, VMEM],
        out_specs=(VMEM,) * pairs,
        out_shape=(shape(size, PANEL),) * pairs,
        compiler_params=params(4),
        cost_estimate=small(),
        name="spread",
    )(row, keep, got)


def add(parts):
    def body(*refs):
        total = refs[0][...]
        for ref in refs[1:-1]:
            total += ref[...]
        refs[-1][...] = total

    return pl.pallas_call(
        body,
        in_specs=[VMEM] * len(parts),
        out_specs=VMEM,
        out_shape=shape(*parts[0].shape),
        compiler_params=params(2),
        cost_estimate=small(),
        name="add",
    )(*parts)


def gram_part(col, row, matrix):
    tiles = 8
    rows = matrix.shape[0] // tiles

    def body(col_ref, row_ref, source, keep, give, held, sems):
        @pl.when(col_ref[0] == 0)
        def _():
            copies = [
                pltpu.make_async_copy(
                    source.at[pl.ds(t * rows, rows), pl.ds(0, PANEL)], held.at[t], sems.at[t]
                )
                for t in range(tiles)
            ]
            for copy in copies:
                copy.start()
            square = jnp.zeros((PANEL, PANEL), F32)
            cross = jnp.zeros((PANEL, PANEL), F32)
            dims = ((0,), (0,))
            for t in range(tiles):
                copies[t].wait()
                high, low = split(held[t])
                square += dot(high, high, dims) + dot(low, low, dims)
                cross += dot(high, low, dims)
            total = square + (cross + cross.T)
            upper = row_ref[0] % 2 == 0
            keep[...] = jnp.where(upper, total[:HALF, :], total[HALF:, :])
            give[...] = jnp.where(upper, total[HALF:, :], total[:HALF, :])

    return pl.pallas_call(
        body,
        in_specs=[SMEM, SMEM, ANY],
        out_specs=(VMEM, VMEM),
        out_shape=(shape(HALF, PANEL),) * 2,
        scratch_shapes=[
            pltpu.VMEM((tiles, rows, PANEL), F32),
            pltpu.SemaphoreType.DMA((tiles,)),
        ],
        compiler_params=params(55),
        cost_estimate=small(),
        name="gram",
    )(col, row, matrix)


def eliminate(col, row, state, block):
    first, last = block * BLOCK, (block + 1) * BLOCK
    width = 2 * PANEL

    def body(col_ref, row_ref, src, *rest):
        out, packed = (rest[-2:] if last == PANEL else (rest[-1], None))

        @pl.when(col_ref[0] == 0)
        def _():
            if block == 0:
                row = lax.broadcasted_iota(jnp.int32, (PANEL, PANEL), 0)
                lane = lax.broadcasted_iota(jnp.int32, (PANEL, PANEL), 1)
                upper = row_ref[0] % 2 == 0
                out[:HALF, :PANEL] = jnp.where(upper, src[...], rest[0][...])
                out[HALF:, :PANEL] = jnp.where(upper, rest[0][...], src[...])
                out[:, PANEL:] = (row == lane).astype(F32)
            else:
                out[...] = src[...]
            row = lax.broadcasted_iota(jnp.int32, (BLOCK, BLOCK), 0)
            lane = lax.broadcasted_iota(jnp.int32, (BLOCK, BLOCK), 1)
            work = jnp.concatenate(
                [out[first:last, first:last], (row == lane).astype(F32)], axis=1
            )
            below = lax.broadcasted_iota(jnp.int32, (BLOCK, 2 * BLOCK), 0)
            scale = jnp.zeros((BLOCK, 2 * BLOCK), F32)
            for i in range(0, BLOCK, 2):
                column = jnp.broadcast_to(work[:, i : i + 1], work.shape)
                follow = jnp.broadcast_to(work[:, i + 1 : i + 2], work.shape)
                upper, lower = work[i : i + 1, :], work[i + 1 : i + 2, :]
                pivot, cross = column[i : i + 1, :], column[i + 1 : i + 2, :]
                inverse = 1.0 / pivot
                ratio = cross * inverse
                second = follow[i + 1 : i + 2, :] - ratio * follow[i : i + 1, :]
                factor = jnp.where(below > i, column * inverse, 0.0)
                follow = follow - factor * follow[i : i + 1, :]
                after = jnp.where(below > i + 1, follow * (1.0 / second), 0.0)
                lower = lower - ratio * upper
                work = work - factor * upper - after * lower
                scale = jnp.where(below == i, pivot, jnp.where(below == i + 1, second, scale))
            root = lax.rsqrt(scale)
            root = root * (1.5 - 0.5 * scale * root * root)
            rows = dot((work * root)[:, BLOCK:], out[first:last, :], ((1,), (0,)), HIGHEST)
            out[first:last, :] = rows
            if last == PANEL:
                packed[:HALF, :] = out[HALF:, PANEL:]
                packed[HALF:, :HALF] = out[: HALF // 2, PANEL : PANEL + HALF]
                packed[HALF:, HALF:] = out[HALF // 2 : HALF, PANEL : PANEL + HALF]
            else:
                left, right = last // 128 * 128, PANEL + -(-last // 128) * 128
                out[last:, left:right] -= dot(
                    rows[:, last:PANEL], rows[:, left:right], ((0,), (0,)), HIGHEST
                )

    return pl.pallas_call(
        body,
        in_specs=[SMEM, SMEM] + [VMEM] * len(state),
        out_specs=(VMEM, VMEM) if last == PANEL else VMEM,
        out_shape=(shape(PANEL, width), shape(HALF + HALF // 2, PANEL))
        if last == PANEL
        else shape(PANEL, width),
        input_output_aliases={2: 0} if block else {},
        compiler_params=params(8),
        cost_estimate=small(),
        name=f"eliminate{block}",
    )(col, row, *state)


def consume(col, row, matrix, sent, step, before, pairs):
    rows, width = sent.shape[0], matrix.shape[1]

    def body(col_ref, row_ref, block, source, *refs):
        if pairs:
            total, _, keep, give, halves, held, sem, turned = refs
        elif step > LAG:
            total, _, out, halves, held, sem = refs
        else:
            out, halves, held, sem = refs
        chunk = step - LAG * col_ref[0]

        def part(first, piece):
            count = piece.shape[0]
            here = pl.ds(pl.multiple_of(first, rows), count)
            high, low = split(piece)
            held[:count, :PANEL] = high
            held[:count, PANEL:] = low
            copy = pltpu.make_async_copy(held.at[pl.ds(0, count), :], halves.at[here, :], sem)
            copy.start()
            a_high, a_low = split(block[here, :])
            dims = ((0,), (0,))
            value = dot(high, a_high, dims) + dot(low, a_high, dims) + dot(high, a_low, dims)
            copy.wait()
            return value

        valid = (col_ref[0] > 0) & (chunk >= 0) & (chunk < CHUNKS)
        if pairs:
            turned[...] = total[...].T

            @pl.when(valid)
            def _():
                turned[...] += part(chunk * rows, source[...]).T

            halve(turned, row_ref, keep, give, pairs)
        else:
            out[...] = total[...] if step > LAG else jnp.zeros_like(out)

            @pl.when(valid)
            def _():
                out[...] += part(chunk * rows, source[...])

            if step == CHUNKS + 1:

                @pl.when(col_ref[0] == 0)
                def _():
                    size = OWN * rows

                    @pl.loop(0, CHUNKS // OWN)
                    def _(k):
                        here = pl.ds(pl.multiple_of(k * size, size), size)
                        out[...] += part(k * size, block[here, :PANEL])

    halves = shape(matrix.shape[0], 2 * PANEL, dtype=BF16)
    if pairs:
        outs = (shape(width // 2, PANEL),) * 2 + (halves,)
    else:
        outs = (shape(PANEL, width), halves)
    return pl.pallas_call(
        body,
        in_specs=[SMEM, SMEM, VMEM, VMEM] + ([VMEM, ANY] if step > LAG else []),
        out_specs=(VMEM,) * (len(outs) - 1) + (ANY,),
        out_shape=outs,
        input_output_aliases={5: len(outs) - 1} if step > LAG else {},
        scratch_shapes=[
            pltpu.VMEM((OWN * rows if step == CHUNKS + 1 else rows, 2 * PANEL), BF16),
            pltpu.SemaphoreType.DMA(()),
        ]
        + ([pltpu.VMEM((width, PANEL), F32)] if pairs else []),
        compiler_params=params(16),
        cost_estimate=small(),
        name="consume",
    )(col, row, matrix, sent, *before)


def solve(col, parts, hops):
    n, rows = len(parts), parts[0].shape[0]
    pieces, size = len(hops[0]), hops[0][0].shape[0]

    def body(col_ref, *refs):
        sources, (top, coeffs, inverse, packed) = refs[n:-4], refs[-4:]
        for h in range(len(hops)):

            @pl.when(col_ref[0] == h)
            def _():
                for p in range(pieces):
                    packed[p * size : (p + 1) * size, :] = sources[h * pieces + p][...]

        inverse[HALF:, :] = packed[:HALF, :]
        inverse[: HALF // 2, :HALF] = packed[HALF : HALF + HALF // 2, :HALF]
        inverse[HALF // 2 : HALF, :HALF] = packed[HALF : HALF + HALF // 2, HALF:]
        inverse[:HALF, HALF:] = jnp.zeros((HALF, HALF), F32)
        total = refs[0][...]
        for ref in refs[1:n]:
            total += ref[...]
        value = dot(total, inverse[...], ((1,), (1,)), HIGHEST)
        top[...] = value
        coeffs[...] = dot(value, inverse[...], ((1,), (0,)), HIGHEST)

    return pl.pallas_call(
        body,
        in_specs=[SMEM] + [VMEM] * (n + len(hops) * pieces),
        out_specs=(VMEM, VMEM),
        out_shape=(shape(rows, PANEL),) * 2,
        scratch_shapes=[pltpu.VMEM((PANEL, PANEL), F32), pltpu.VMEM((pieces * size, PANEL), F32)],
        compiler_params=params(6),
        cost_estimate=small(),
        name="solve",
    )(col, *parts, *[piece for hop in hops for piece in hop])


def subtract(matrix, halves, coeffs):
    rows, width = matrix.shape
    tiles = 12
    size = rows // tiles

    def body(a, p, c, out, ct, held, sems):
        ct_high, ct_low = split(c[...].T)
        ct[:PANEL, :] = ct_high
        ct[PANEL : 2 * PANEL, :] = ct_high
        ct[2 * PANEL :, :] = ct_low
        copies = [
            pltpu.make_async_copy(held.at[t], out.at[pl.ds(t * size, size), :], sems.at[t])
            for t in range(tiles)
        ]
        for t in range(tiles):
            here = slice(t * size, (t + 1) * size)
            both = p[here, :]
            thrice = jnp.concatenate([both, both[:, :PANEL]], axis=1)
            value = a[here, :] - dot(thrice, ct[...], ((1,), (0,)))
            held[t] = value
            copies[t].start()
        for copy in copies:
            copy.wait()

    return pl.pallas_call(
        body,
        in_specs=[VMEM] * 3,
        out_specs=ANY,
        out_shape=shape(rows, width),
        scratch_shapes=[
            pltpu.VMEM((3 * PANEL, width), BF16),
            pltpu.VMEM((tiles, size, width), F32),
            pltpu.SemaphoreType.DMA((tiles,)),
        ],
        compiler_params=params(20),
        cost_estimate=small(),
        name="subtract",
    )(matrix, halves, coeffs)


def program(n_row, n_col):
    pairs = n_row // 2

    def swap(x, bit):
        return lax.ppermute(x, "row", [(r, r ^ bit) for r in range(n_row)])

    def scatter(row, keep, give):
        parts = spread(row, keep, swap(give, 1), pairs)
        return [parts[0]] + [swap(parts[j], 2 * j) for j in reversed(range(1, pairs))]

    def shards(matrix):
        col = lax.axis_index("col").astype(jnp.int32).reshape(1)
        row = lax.axis_index("row").astype(jnp.int32).reshape(1)
        blocks = PANEL // BLOCK
        rows = matrix.shape[0] // CHUNKS
        pieces = -(-(HALF + HALF // 2) // rows)
        shifts = CHUNKS + pieces + LAG * (n_col - 2)
        last = CHUNKS - 1 + LAG * (n_col - 1)
        first = LAG + 3
        due = [first + i * (CHUNKS - 1 - first) // (blocks - 1) for i in range(blocks)]
        sent, received, sums = [], [], {}
        half = state = packed = None
        for s in range(shifts + LAG):
            if s < LAG:
                sent.append(matrix[s * rows : (s + 1) * rows, :PANEL])
            elif s < shifts:
                after = [sums[s - 2 * LAG][0]] if s - 2 * LAG in sums else []
                if s == LAG:
                    keep, give = gram_part(col, row, matrix)
                    half = add([keep, swap(give, 1)])
                elif state is not None:
                    after.append(state[0])
                x = received[s - LAG]
                if s < CHUNKS:
                    sent.append(fill(col, x, matrix, s * rows, *after))
                elif s < CHUNKS + pieces:
                    sent.append(fill(col, x, packed, (s - CHUNKS) * rows, *after))
                else:
                    sent.append(gate(x, *after))
            else:
                sent.append(received[s - LAG])
            if s < shifts:
                hops = [(h, h + 1) for h in range(n_col - 1) if 0 <= s - LAG * h < CHUNKS + pieces]
                received.append(lax.ppermute(sent[s], "col", hops))
            if LAG <= s <= last:
                before = sums[s - 1] if s > LAG else ()
                sums[s] = consume(
                    col, row, matrix, sent[s], s, before, pairs if s == last else 0
                )
            if s == LAG + 1:
                half = gate(half, sent[LAG])
                state = [add([half] + [swap(half, 2 * j) for j in range(1, pairs)])]
            elif s == LAG + 2:
                mine = gate(state[0], sent[s])
                state = [mine, swap(mine, 1)]
            elif s in due:
                block = due.index(s)
                state = eliminate(col, row, [gate(state[0], sent[s]), *state[1:]], block)
                if block == blocks - 1:
                    state, packed = [state[0]], state[1]
                else:
                    state = [state]
        keep, give, halves = sums[last]
        parts = scatter(row, keep, give)
        inverse = [
            [sent[CHUNKS + p + LAG * h] for p in range(pieces)] for h in range(n_col)
        ]
        top_rows, coeffs = solve(col, parts, inverse)
        coeffs = lax.all_gather(coeffs, "row", axis=0, tiled=True)
        return top_rows, subtract(matrix, halves, coeffs)

    return shards


def solution(mesh):
    return jax.shard_map(
        program(mesh.shape["row"], mesh.shape["col"]),
        mesh=mesh,
        in_specs=(P("row", "col"),),
        out_specs=(P(("col", "row"), None), P("row", "col")),
        check_vma=False,
    )
```

```python
import jax
import jax.numpy as jnp
from jax import lax
from jax.experimental import pallas as pl
from jax.experimental.pallas import tpu as pltpu
from jax.sharding import PartitionSpec as P

PANEL = 256
CHUNKS = 16
LAG = 3
HALF = PANEL // 2
OWN = 4
BLOCK = 32
HIGHEST = lax.Precision.HIGHEST
F32, BF16 = jnp.float32, jnp.bfloat16
ANY = pl.BlockSpec(memory_space=pl.ANY)
SMEM = pl.BlockSpec(memory_space=pltpu.SMEM)
VMEM = pl.BlockSpec(memory_space=pltpu.VMEM)


def params(mib):
    return pltpu.CompilerParams(vmem_limit_bytes=mib * 1024 * 1024)


def small():
    return pl.CostEstimate(flops=1, bytes_accessed=1, transcendentals=0)


def shape(*dims, dtype=F32):
    return jax.ShapeDtypeStruct(dims, dtype)


def split(x):
    hi = x.astype(BF16)
    return hi, (x - hi.astype(F32)).astype(BF16)


def dot(a, b, dims, precision=None):
    return lax.dot_general(
        a, b, (dims, ((), ())), precision=precision, preferred_element_type=F32
    )


def gate(x, *after):
    def body(*refs):
        pass

    return pl.pallas_call(
        body,
        in_specs=[ANY] * (1 + len(after)),
        out_specs=ANY,
        out_shape=shape(*x.shape, dtype=x.dtype),
        input_output_aliases={0: 0},
        compiler_params=params(1),
        cost_estimate=small(),
        name="gate",
    )(x, *after)


def fill(col, received, source, first, *after):
    rows = min(received.shape[0], source.shape[0] - first)

    def body(col_ref, _, source_ref, *refs):
        out, sem = refs[-2:]

        @pl.when(col_ref[0] == 0)
        def _():
            own = source_ref.at[pl.ds(first, rows), pl.ds(0, PANEL)]
            copy = pltpu.make_async_copy(own, out.at[pl.ds(0, rows), :], sem)
            copy.start()
            copy.wait()

    return pl.pallas_call(
        body,
        in_specs=[SMEM] + [ANY] * (2 + len(after)),
        out_specs=ANY,
        out_shape=shape(*received.shape),
        input_output_aliases={1: 0},
        scratch_shapes=[pltpu.SemaphoreType.DMA(())],
        compiler_params=params(1),
        cost_estimate=small(),
        name="fill",
    )(col, received, source, *after)


def halve(total, row_ref, keep, give, pairs):
    size = total.shape[0] // (2 * pairs)
    core = row_ref[0] % 2
    for k in range(pairs):
        here = slice(k * size, (k + 1) * size)
        mine = pl.multiple_of((2 * k + core) * size, size)
        other = pl.multiple_of((2 * k + 1 - core) * size, size)
        keep[here, :] = total[pl.ds(mine, size), :]
        give[here, :] = total[pl.ds(other, size), :]


def spread(row, keep, got, pairs):
    size = keep.shape[0] // pairs

    def body(row_ref, keep_ref, got_ref, *outs):
        chip = row_ref[0] // 2
        for j, out in enumerate(outs):
            here = pl.ds(pl.multiple_of((chip ^ j) * size, size), size)
            out[...] = keep_ref[here, :] + got_ref[here, :]

    return pl.pallas_call(
        body,
        in_specs=[SMEM, VMEM, VMEM],
        out_specs=(VMEM,) * pairs,
        out_shape=(shape(size, PANEL),) * pairs,
        compiler_params=params(4),
        cost_estimate=small(),
        name="spread",
    )(row, keep, got)


def add(parts):
    def body(*refs):
        total = refs[0][...]
        for ref in refs[1:-1]:
            total += ref[...]
        refs[-1][...] = total

    return pl.pallas_call(
        body,
        in_specs=[VMEM] * len(parts),
        out_specs=VMEM,
        out_shape=shape(*parts[0].shape),
        compiler_params=params(2),
        cost_estimate=small(),
        name="add",
    )(*parts)


def gram_part(col, row, matrix):
    tiles = 8
    rows = matrix.shape[0] // tiles

    def body(col_ref, row_ref, source, keep, give, held, sems):
        @pl.when(col_ref[0] == 0)
        def _():
            copies = [
                pltpu.make_async_copy(
                    source.at[pl.ds(t * rows, rows), pl.ds(0, PANEL)], held.at[t], sems.at[t]
                )
                for t in range(tiles)
            ]
            for copy in copies:
                copy.start()
            square = jnp.zeros((PANEL, PANEL), F32)
            cross = jnp.zeros((PANEL, PANEL), F32)
            dims = ((0,), (0,))
            for t in range(tiles):
                copies[t].wait()
                high, low = split(held[t])
                square += dot(high, high, dims) + dot(low, low, dims)
                cross += dot(high, low, dims)
            total = square + (cross + cross.T)
            upper = row_ref[0] % 2 == 0
            keep[...] = jnp.where(upper, total[:HALF, :], total[HALF:, :])
            give[...] = jnp.where(upper, total[HALF:, :], total[:HALF, :])

    return pl.pallas_call(
        body,
        in_specs=[SMEM, SMEM, ANY],
        out_specs=(VMEM, VMEM),
        out_shape=(shape(HALF, PANEL),) * 2,
        scratch_shapes=[
            pltpu.VMEM((tiles, rows, PANEL), F32),
            pltpu.SemaphoreType.DMA((tiles,)),
        ],
        compiler_params=params(55),
        cost_estimate=small(),
        name="gram",
    )(col, row, matrix)


def eliminate(col, row, state, block):
    first, last = block * BLOCK, (block + 1) * BLOCK
    width = 2 * PANEL

    def body(col_ref, row_ref, src, *rest):
        out, packed = (rest[-2:] if last == PANEL else (rest[-1], None))

        @pl.when(col_ref[0] == 0)
        def _():
            if block == 0:
                row = lax.broadcasted_iota(jnp.int32, (PANEL, PANEL), 0)
                lane = lax.broadcasted_iota(jnp.int32, (PANEL, PANEL), 1)
                upper = row_ref[0] % 2 == 0
                out[:HALF, :PANEL] = jnp.where(upper, src[...], rest[0][...])
                out[HALF:, :PANEL] = jnp.where(upper, rest[0][...], src[...])
                out[:, PANEL:] = (row == lane).astype(F32)
            else:
                out[...] = src[...]
            row = lax.broadcasted_iota(jnp.int32, (BLOCK, BLOCK), 0)
            lane = lax.broadcasted_iota(jnp.int32, (BLOCK, BLOCK), 1)
            work = jnp.concatenate(
                [out[first:last, first:last], (row == lane).astype(F32)], axis=1
            )
            below = lax.broadcasted_iota(jnp.int32, (BLOCK, 2 * BLOCK), 0)
            scale = jnp.zeros((BLOCK, 2 * BLOCK), F32)
            for i in range(0, BLOCK, 2):
                column = jnp.broadcast_to(work[:, i : i + 1], work.shape)
                follow = jnp.broadcast_to(work[:, i + 1 : i + 2], work.shape)
                upper, lower = work[i : i + 1, :], work[i + 1 : i + 2, :]
                pivot, cross = column[i : i + 1, :], column[i + 1 : i + 2, :]
                inverse = 1.0 / pivot
                ratio = cross * inverse
                second = follow[i + 1 : i + 2, :] - ratio * follow[i : i + 1, :]
                factor = jnp.where(below > i, column * inverse, 0.0)
                follow = follow - factor * follow[i : i + 1, :]
                after = jnp.where(below > i + 1, follow * (1.0 / second), 0.0)
                lower = lower - ratio * upper
                work = work - factor * upper - after * lower
                scale = jnp.where(below == i, pivot, jnp.where(below == i + 1, second, scale))
            root = lax.rsqrt(scale)
            root = root * (1.5 - 0.5 * scale * root * root)
            rows = dot((work * root)[:, BLOCK:], out[first:last, :], ((1,), (0,)), HIGHEST)
            out[first:last, :] = rows
            if last == PANEL:
                packed[:HALF, :] = out[HALF:, PANEL:]
                packed[HALF:, :HALF] = out[: HALF // 2, PANEL : PANEL + HALF]
                packed[HALF:, HALF:] = out[HALF // 2 : HALF, PANEL : PANEL + HALF]
            else:
                left, right = last // 128 * 128, PANEL + -(-last // 128) * 128
                out[last:, left:right] -= dot(
                    rows[:, last:PANEL], rows[:, left:right], ((0,), (0,)), HIGHEST
                )

    return pl.pallas_call(
        body,
        in_specs=[SMEM, SMEM] + [VMEM] * len(state),
        out_specs=(VMEM, VMEM) if last == PANEL else VMEM,
        out_shape=(shape(PANEL, width), shape(HALF + HALF // 2, PANEL))
        if last == PANEL
        else shape(PANEL, width),
        input_output_aliases={2: 0} if block else {},
        compiler_params=params(8),
        cost_estimate=small(),
        name=f"eliminate{block}",
    )(col, row, *state)


def consume(col, row, matrix, sent, step, before, pairs):
    rows, width = sent.shape[0], matrix.shape[1]

    def body(col_ref, row_ref, block, source, *refs):
        if pairs:
            total, _, keep, give, halves, held, sem, turned = refs
        elif step > LAG:
            total, _, out, halves, held, sem = refs
        else:
            out, halves, held, sem = refs
        chunk = step - LAG * col_ref[0]

        def part(first, piece):
            count = piece.shape[0]
            here = pl.ds(pl.multiple_of(first, rows), count)
            high, low = split(piece)
            held[:count, :PANEL] = high
            held[:count, PANEL:] = low
            copy = pltpu.make_async_copy(held.at[pl.ds(0, count), :], halves.at[here, :], sem)
            copy.start()
            a_high, a_low = split(block[here, :])
            dims = ((0,), (0,))
            value = dot(high, a_high, dims) + dot(low, a_high, dims) + dot(high, a_low, dims)
            copy.wait()
            return value

        valid = (col_ref[0] > 0) & (chunk >= 0) & (chunk < CHUNKS)
        if pairs:
            turned[...] = total[...].T

            @pl.when(valid)
            def _():
                turned[...] += part(chunk * rows, source[...]).T

            halve(turned, row_ref, keep, give, pairs)
        else:
            out[...] = total[...] if step > LAG else jnp.zeros_like(out)

            @pl.when(valid)
            def _():
                out[...] += part(chunk * rows, source[...])

            if step == CHUNKS + 1:

                @pl.when(col_ref[0] == 0)
                def _():
                    size = OWN * rows

                    @pl.loop(0, CHUNKS // OWN)
                    def _(k):
                        here = pl.ds(pl.multiple_of(k * size, size), size)
                        out[...] += part(k * size, block[here, :PANEL])

    halves = shape(matrix.shape[0], 2 * PANEL, dtype=BF16)
    if pairs:
        outs = (shape(width // 2, PANEL),) * 2 + (halves,)
    else:
        outs = (shape(PANEL, width), halves)
    return pl.pallas_call(
        body,
        in_specs=[SMEM, SMEM, VMEM, VMEM] + ([VMEM, ANY] if step > LAG else []),
        out_specs=(VMEM,) * (len(outs) - 1) + (ANY,),
        out_shape=outs,
        input_output_aliases={5: len(outs) - 1} if step > LAG else {},
        scratch_shapes=[
            pltpu.VMEM((OWN * rows if step == CHUNKS + 1 else rows, 2 * PANEL), BF16),
            pltpu.SemaphoreType.DMA(()),
        ]
        + ([pltpu.VMEM((width, PANEL), F32)] if pairs else []),
        compiler_params=params(16),
        cost_estimate=small(),
        name="consume",
    )(col, row, matrix, sent, *before)


def solve(col, parts, hops):
    n, rows = len(parts), parts[0].shape[0]
    pieces, size = len(hops[0]), hops[0][0].shape[0]

    def body(col_ref, *refs):
        sources, (top, coeffs, inverse, packed) = refs[n:-4], refs[-4:]
        for h in range(len(hops)):

            @pl.when(col_ref[0] == h)
            def _():
                for p in range(pieces):
                    packed[p * size : (p + 1) * size, :] = sources[h * pieces + p][...]

        inverse[HALF:, :] = packed[:HALF, :]
        inverse[: HALF // 2, :HALF] = packed[HALF : HALF + HALF // 2, :HALF]
        inverse[HALF // 2 : HALF, :HALF] = packed[HALF : HALF + HALF // 2, HALF:]
        inverse[:HALF, HALF:] = jnp.zeros((HALF, HALF), F32)
        total = refs[0][...]
        for ref in refs[1:n]:
            total += ref[...]
        value = dot(total, inverse[...], ((1,), (1,)), HIGHEST)
        top[...] = value
        coeffs[...] = dot(value, inverse[...], ((1,), (0,)), HIGHEST)

    return pl.pallas_call(
        body,
        in_specs=[SMEM] + [VMEM] * (n + len(hops) * pieces),
        out_specs=(VMEM, VMEM),
        out_shape=(shape(rows, PANEL),) * 2,
        scratch_shapes=[pltpu.VMEM((PANEL, PANEL), F32), pltpu.VMEM((pieces * size, PANEL), F32)],
        compiler_params=params(6),
        cost_estimate=small(),
        name="solve",
    )(col, *parts, *[piece for hop in hops for piece in hop])


def stack(parts):
    size = parts[0].shape[0]

    def body(*refs):
        for k, ref in enumerate(refs[:-1]):
            refs[-1][k * size : (k + 1) * size, :] = ref[...]

    return pl.pallas_call(
        body,
        in_specs=[VMEM] * len(parts),
        out_specs=VMEM,
        out_shape=shape(len(parts) * size, PANEL),
        compiler_params=params(4),
        cost_estimate=small(),
        name="stack",
    )(*parts)


def subtract(row, matrix, halves, mine, other, pairs):
    rows, width = matrix.shape
    tiles = 12
    size = rows // tiles
    block = width // (2 * pairs)

    def body(row_ref, a, p, mine_ref, other_ref, out, coeffs, ct, held, sems):
        chip, first = row_ref[0] // 2, row_ref[0] % 2 == 0
        for k in range(pairs):
            here = pl.ds(pl.multiple_of((chip ^ k) * block, block), block)
            one, two = mine_ref[here, :], other_ref[here, :]
            coeffs[2 * k * block : (2 * k + 1) * block, :] = jnp.where(first, one, two)
            coeffs[(2 * k + 1) * block : (2 * k + 2) * block, :] = jnp.where(first, two, one)
        ct_high, ct_low = split(coeffs[...].T)
        ct[:PANEL, :] = ct_high
        ct[PANEL : 2 * PANEL, :] = ct_high
        ct[2 * PANEL :, :] = ct_low
        copies = [
            pltpu.make_async_copy(held.at[t], out.at[pl.ds(t * size, size), :], sems.at[t])
            for t in range(tiles)
        ]
        for t in range(tiles):
            here = slice(t * size, (t + 1) * size)
            both = p[here, :]
            thrice = jnp.concatenate([both, both[:, :PANEL]], axis=1)
            value = a[here, :] - dot(thrice, ct[...], ((1,), (0,)))
            held[t] = value
            copies[t].start()
        for copy in copies:
            copy.wait()

    return pl.pallas_call(
        body,
        in_specs=[SMEM] + [VMEM] * 4,
        out_specs=ANY,
        out_shape=shape(rows, width),
        scratch_shapes=[
            pltpu.VMEM((width, PANEL), F32),
            pltpu.VMEM((3 * PANEL, width), BF16),
            pltpu.VMEM((tiles, size, width), F32),
            pltpu.SemaphoreType.DMA((tiles,)),
        ],
        compiler_params=params(22),
        cost_estimate=small(),
        name="subtract",
    )(row, matrix, halves, mine, other)


def program(n_row, n_col):
    pairs = n_row // 2

    def swap(x, bit):
        return lax.ppermute(x, "row", [(r, r ^ bit) for r in range(n_row)])

    def scatter(row, keep, give):
        parts = spread(row, keep, swap(give, 1), pairs)
        return [parts[0]] + [swap(parts[j], 2 * j) for j in reversed(range(1, pairs))]

    def shards(matrix):
        col = lax.axis_index("col").astype(jnp.int32).reshape(1)
        row = lax.axis_index("row").astype(jnp.int32).reshape(1)
        blocks = PANEL // BLOCK
        rows = matrix.shape[0] // CHUNKS
        pieces = -(-(HALF + HALF // 2) // rows)
        shifts = CHUNKS + pieces + LAG * (n_col - 2)
        last = CHUNKS - 1 + LAG * (n_col - 1)
        first = LAG + 3
        due = [first + i * (CHUNKS - 1 - first) // (blocks - 1) for i in range(blocks)]
        sent, received, sums = [], [], {}
        half = state = packed = None
        for s in range(shifts + LAG):
            if s < LAG:
                sent.append(matrix[s * rows : (s + 1) * rows, :PANEL])
            elif s < shifts:
                after = [sums[s - 2 * LAG][0]] if s - 2 * LAG in sums else []
                if s == LAG:
                    keep, give = gram_part(col, row, matrix)
                    half = add([keep, swap(give, 1)])
                elif state is not None:
                    after.append(state[0])
                x = received[s - LAG]
                if s < CHUNKS:
                    sent.append(fill(col, x, matrix, s * rows, *after))
                elif s < CHUNKS + pieces:
                    sent.append(fill(col, x, packed, (s - CHUNKS) * rows, *after))
                else:
                    sent.append(gate(x, *after))
            else:
                sent.append(received[s - LAG])
            if s < shifts:
                hops = [(h, h + 1) for h in range(n_col - 1) if 0 <= s - LAG * h < CHUNKS + pieces]
                received.append(lax.ppermute(sent[s], "col", hops))
            if LAG <= s <= last:
                before = sums[s - 1] if s > LAG else ()
                sums[s] = consume(
                    col, row, matrix, sent[s], s, before, pairs if s == last else 0
                )
            if s == LAG + 1:
                half = gate(half, sent[LAG])
                state = [add([half] + [swap(half, 2 * j) for j in range(1, pairs)])]
            elif s == LAG + 2:
                mine = gate(state[0], sent[s])
                state = [mine, swap(mine, 1)]
            elif s in due:
                block = due.index(s)
                state = eliminate(col, row, [gate(state[0], sent[s]), *state[1:]], block)
                if block == blocks - 1:
                    state, packed = [state[0]], state[1]
                else:
                    state = [state]
        keep, give, halves = sums[last]
        parts = scatter(row, keep, give)
        inverse = [
            [sent[CHUNKS + p + LAG * h] for p in range(pieces)] for h in range(n_col)
        ]
        top_rows, coeffs = solve(col, parts, inverse)
        far = [swap(coeffs, 2 * j) for j in reversed(range(1, pairs))]
        mine = stack([coeffs] + far[::-1])
        return top_rows, subtract(row, matrix, halves, mine, swap(mine, 1), pairs)

    return shards


def solution(mesh):
    return jax.shard_map(
        program(mesh.shape["row"], mesh.shape["col"]),
        mesh=mesh,
        in_specs=(P("row", "col"),),
        out_specs=(P(("col", "row"), None), P("row", "col")),
        check_vma=False,
    )
```

```python
import jax
import jax.numpy as jnp
from jax import lax
from jax.experimental import pallas as pl
from jax.experimental.pallas import tpu as pltpu
from jax.sharding import PartitionSpec as P

PANEL = 256
CHUNKS = 16
LAG = 3
HALF = PANEL // 2
QUARTER = PANEL // 4
PACKED = 2 * QUARTER + QUARTER // 2
OWN = 4
BLOCK = 32
HIGHEST = lax.Precision.HIGHEST
F32, BF16 = jnp.float32, jnp.bfloat16
ANY = pl.BlockSpec(memory_space=pl.ANY)
SMEM = pl.BlockSpec(memory_space=pltpu.SMEM)
VMEM = pl.BlockSpec(memory_space=pltpu.VMEM)


def params(mib):
    return pltpu.CompilerParams(vmem_limit_bytes=mib * 1024 * 1024)


def small():
    return pl.CostEstimate(flops=1, bytes_accessed=1, transcendentals=0)


def shape(*dims, dtype=F32):
    return jax.ShapeDtypeStruct(dims, dtype)


def split(x):
    hi = x.astype(BF16)
    return hi, (x - hi.astype(F32)).astype(BF16)


def dot(a, b, dims, precision=None):
    return lax.dot_general(
        a, b, (dims, ((), ())), precision=precision, preferred_element_type=F32
    )


def gate(x, *after):
    def body(*refs):
        pass

    return pl.pallas_call(
        body,
        in_specs=[ANY] * (1 + len(after)),
        out_specs=ANY,
        out_shape=shape(*x.shape, dtype=x.dtype),
        input_output_aliases={0: 0},
        compiler_params=params(1),
        cost_estimate=small(),
        name="gate",
    )(x, *after)


def fill(col, received, source, first, *after):
    rows = min(received.shape[0], source.shape[0] - first)

    def body(col_ref, _, source_ref, *refs):
        out, sem = refs[-2:]

        @pl.when(col_ref[0] == 0)
        def _():
            own = source_ref.at[pl.ds(first, rows), pl.ds(0, PANEL)]
            copy = pltpu.make_async_copy(own, out.at[pl.ds(0, rows), :], sem)
            copy.start()
            copy.wait()

    return pl.pallas_call(
        body,
        in_specs=[SMEM] + [ANY] * (2 + len(after)),
        out_specs=ANY,
        out_shape=shape(*received.shape),
        input_output_aliases={1: 0},
        scratch_shapes=[pltpu.SemaphoreType.DMA(())],
        compiler_params=params(1),
        cost_estimate=small(),
        name="fill",
    )(col, received, source, *after)


def halve(total, row_ref, keep, give, pairs):
    size = total.shape[0] // (2 * pairs)
    core = row_ref[0] % 2
    for k in range(pairs):
        here = slice(k * size, (k + 1) * size)
        mine = pl.multiple_of((2 * k + core) * size, size)
        other = pl.multiple_of((2 * k + 1 - core) * size, size)
        keep[here, :] = total[pl.ds(mine, size), :]
        give[here, :] = total[pl.ds(other, size), :]


def spread(row, keep, got, pairs):
    size = keep.shape[0] // pairs

    def body(row_ref, keep_ref, got_ref, *outs):
        chip = row_ref[0] // 2
        for j, out in enumerate(outs):
            here = pl.ds(pl.multiple_of((chip ^ j) * size, size), size)
            out[...] = keep_ref[here, :] + got_ref[here, :]

    return pl.pallas_call(
        body,
        in_specs=[SMEM, VMEM, VMEM],
        out_specs=(VMEM,) * pairs,
        out_shape=(shape(size, PANEL),) * pairs,
        compiler_params=params(4),
        cost_estimate=small(),
        name="spread",
    )(row, keep, got)


def add(parts):
    def body(*refs):
        total = refs[0][...]
        for ref in refs[1:-1]:
            total += ref[...]
        refs[-1][...] = total

    return pl.pallas_call(
        body,
        in_specs=[VMEM] * len(parts),
        out_specs=VMEM,
        out_shape=shape(*parts[0].shape),
        compiler_params=params(2),
        cost_estimate=small(),
        name="add",
    )(*parts)


def gram_part(col, row, matrix):
    tiles = 8
    rows = matrix.shape[0] // tiles

    def body(col_ref, row_ref, source, keep, give, held, sems):
        @pl.when(col_ref[0] == 0)
        def _():
            copies = [
                pltpu.make_async_copy(
                    source.at[pl.ds(t * rows, rows), pl.ds(0, PANEL)], held.at[t], sems.at[t]
                )
                for t in range(tiles)
            ]
            for copy in copies:
                copy.start()
            square = jnp.zeros((PANEL, PANEL), F32)
            cross = jnp.zeros((PANEL, PANEL), F32)
            dims = ((0,), (0,))
            for t in range(tiles):
                copies[t].wait()
                high, low = split(held[t])
                square += dot(high, high, dims) + dot(low, low, dims)
                cross += dot(high, low, dims)
            total = square + (cross + cross.T)
            upper = row_ref[0] % 2 == 0
            keep[...] = jnp.where(upper, total[:HALF, :], total[HALF:, :])
            give[...] = jnp.where(upper, total[HALF:, :], total[:HALF, :])

    return pl.pallas_call(
        body,
        in_specs=[SMEM, SMEM, ANY],
        out_specs=(VMEM, VMEM),
        out_shape=(shape(HALF, PANEL),) * 2,
        scratch_shapes=[
            pltpu.VMEM((tiles, rows, PANEL), F32),
            pltpu.SemaphoreType.DMA((tiles,)),
        ],
        compiler_params=params(53),
        cost_estimate=small(),
        name="gram",
    )(col, row, matrix)


def eliminate(col, row, state, block):
    first, last = block * BLOCK, (block + 1) * BLOCK
    width = 2 * PANEL

    def body(col_ref, row_ref, src, *rest):
        out, packed = (rest[-2:] if last == PANEL else (rest[-1], None))

        @pl.when(col_ref[0] == 0)
        def _():
            if block == 0:
                row = lax.broadcasted_iota(jnp.int32, (PANEL, PANEL), 0)
                lane = lax.broadcasted_iota(jnp.int32, (PANEL, PANEL), 1)
                upper = row_ref[0] % 2 == 0
                out[:HALF, :PANEL] = jnp.where(upper, src[...], rest[0][...])
                out[HALF:, :PANEL] = jnp.where(upper, rest[0][...], src[...])
                out[:, PANEL:] = (row == lane).astype(F32)
            else:
                out[...] = src[...]
            row = lax.broadcasted_iota(jnp.int32, (BLOCK, BLOCK), 0)
            lane = lax.broadcasted_iota(jnp.int32, (BLOCK, BLOCK), 1)
            work = jnp.concatenate(
                [out[first:last, first:last], (row == lane).astype(F32)], axis=1
            )
            below = lax.broadcasted_iota(jnp.int32, (BLOCK, 2 * BLOCK), 0)
            scale = jnp.zeros((BLOCK, 2 * BLOCK), F32)
            for i in range(0, BLOCK, 2):
                column = jnp.broadcast_to(work[:, i : i + 1], work.shape)
                follow = jnp.broadcast_to(work[:, i + 1 : i + 2], work.shape)
                upper, lower = work[i : i + 1, :], work[i + 1 : i + 2, :]
                pivot, cross = column[i : i + 1, :], column[i + 1 : i + 2, :]
                inverse = 1.0 / pivot
                ratio = cross * inverse
                second = follow[i + 1 : i + 2, :] - ratio * follow[i : i + 1, :]
                factor = jnp.where(below > i, column * inverse, 0.0)
                follow = follow - factor * follow[i : i + 1, :]
                after = jnp.where(below > i + 1, follow * (1.0 / second), 0.0)
                lower = lower - ratio * upper
                work = work - factor * upper - after * lower
                scale = jnp.where(below == i, pivot, jnp.where(below == i + 1, second, scale))
            root = lax.rsqrt(scale)
            root = root * (1.5 - 0.5 * scale * root * root)
            rows = dot((work * root)[:, BLOCK:], out[first:last, :], ((1,), (0,)), HIGHEST)
            out[first:last, :] = rows
            if last == PANEL:
                q = QUARTER
                packed[:q, :] = out[3 * q :, PANEL:]
                packed[q : 2 * q, : 3 * q] = out[2 * q : 3 * q, PANEL : PANEL + 3 * q]
                packed[q : 2 * q, 3 * q :] = out[:q, PANEL : PANEL + q]
                for k in range(4):
                    high, left = q + k % 2 * (q // 2), PANEL + k // 2 * q
                    packed[2 * q :, k * q : (k + 1) * q] = out[high : high + q // 2, left : left + q]
            else:
                left, right = last // 128 * 128, PANEL + -(-last // 128) * 128
                out[last:, left:right] -= dot(
                    rows[:, last:PANEL], rows[:, left:right], ((0,), (0,)), HIGHEST
                )

    return pl.pallas_call(
        body,
        in_specs=[SMEM, SMEM] + [VMEM] * len(state),
        out_specs=(VMEM, VMEM) if last == PANEL else VMEM,
        out_shape=(shape(PANEL, width), shape(PACKED, PANEL))
        if last == PANEL
        else shape(PANEL, width),
        input_output_aliases={2: 0} if block else {},
        compiler_params=params(8),
        cost_estimate=small(),
        name=f"eliminate{block}",
    )(col, row, *state)


def consume(col, row, matrix, sent, step, before, pairs):
    rows, width = sent.shape[0], matrix.shape[1]

    def body(col_ref, row_ref, block, source, *refs):
        if pairs:
            total, _, keep, give, halves, held, sem, summed, turned = refs
        elif step > LAG:
            total, _, out, halves, held, sem = refs
        else:
            out, halves, held, sem = refs
        chunk = step - LAG * col_ref[0]

        def part(first, piece):
            count = piece.shape[0]
            here = pl.ds(pl.multiple_of(first, rows), count)
            high, low = split(piece)
            held[:count, :PANEL] = high
            held[:count, PANEL:] = low
            copy = pltpu.make_async_copy(held.at[pl.ds(0, count), :], halves.at[here, :], sem)
            copy.start()
            a_high, a_low = split(block[here, :])
            dims = ((0,), (0,))
            value = dot(high, a_high, dims) + dot(low, a_high, dims) + dot(high, a_low, dims)
            copy.wait()
            return value

        valid = (col_ref[0] > 0) & (chunk >= 0) & (chunk < CHUNKS)
        if pairs:
            summed[...] = total[...]

            @pl.when(valid)
            def _():
                summed[...] += part(chunk * rows, source[...])

            turned[...] = summed[...].T
            halve(turned, row_ref, keep, give, pairs)
        else:
            out[...] = total[...] if step > LAG else jnp.zeros_like(out)

            @pl.when(valid)
            def _():
                out[...] += part(chunk * rows, source[...])

            if step == CHUNKS + 1:

                @pl.when(col_ref[0] == 0)
                def _():
                    size = OWN * rows

                    @pl.loop(0, CHUNKS // OWN)
                    def _(k):
                        here = pl.ds(pl.multiple_of(k * size, size), size)
                        out[...] += part(k * size, block[here, :PANEL])

    halves = shape(matrix.shape[0], 2 * PANEL, dtype=BF16)
    if pairs:
        outs = (shape(width // 2, PANEL),) * 2 + (halves,)
    else:
        outs = (shape(PANEL, width), halves)
    return pl.pallas_call(
        body,
        in_specs=[SMEM, SMEM, VMEM, VMEM] + ([VMEM, ANY] if step > LAG else []),
        out_specs=(VMEM,) * (len(outs) - 1) + (ANY,),
        out_shape=outs,
        input_output_aliases={5: len(outs) - 1} if step > LAG else {},
        scratch_shapes=[
            pltpu.VMEM((OWN * rows if step == CHUNKS + 1 else rows, 2 * PANEL), BF16),
            pltpu.SemaphoreType.DMA(()),
        ]
        + ([pltpu.VMEM(dims, F32) for dims in ((PANEL, width), (width, PANEL))] if pairs else []),
        compiler_params=params(16),
        cost_estimate=small(),
        name="consume",
    )(col, row, matrix, sent, *before)


def cut(col, x, where):
    def body(col_ref, source, out):
        @pl.when(col_ref[0] == where)
        def _():
            out[...] = source[:PACKED, :]

    return pl.pallas_call(
        body,
        in_specs=[SMEM, VMEM],
        out_specs=VMEM,
        out_shape=shape(PACKED, PANEL),
        compiler_params=params(2),
        cost_estimate=small(),
        name="cut",
    )(col, x)


def solve(col, parts, hops):
    n, rows = len(parts), parts[0].shape[0]

    def body(col_ref, *refs):
        sources, (top, coeffs, inverse) = refs[n:-3], refs[-3:]
        q = QUARTER
        inverse[:HALF, HALF:] = jnp.zeros((HALF, HALF), F32)
        inverse[:q, q:HALF] = jnp.zeros((q, q), F32)
        inverse[HALF : 3 * q, 3 * q :] = jnp.zeros((q, q), F32)
        for h, source in enumerate(sources):

            @pl.when(col_ref[0] == h)
            def _():
                inverse[3 * q :, :] = source[:q, :]
                inverse[2 * q : 3 * q, : 3 * q] = source[q : 2 * q, : 3 * q]
                inverse[:q, :q] = source[q : 2 * q, 3 * q :]
                for k in range(4):
                    high, left = q + k % 2 * (q // 2), k // 2 * q
                    piece = source[2 * q : PACKED, k * q : (k + 1) * q]
                    inverse[high : high + q // 2, left : left + q] = piece

        total = refs[0][...]
        for ref in refs[1:n]:
            total += ref[...]
        value = dot(total, inverse[...], ((1,), (1,)), HIGHEST)
        top[...] = value
        coeffs[...] = dot(value, inverse[...], ((1,), (0,)), HIGHEST)

    return pl.pallas_call(
        body,
        in_specs=[SMEM] + [VMEM] * (n + len(hops)),
        out_specs=(VMEM, VMEM),
        out_shape=(shape(rows, PANEL),) * 2,
        scratch_shapes=[pltpu.VMEM((PANEL, PANEL), F32)],
        compiler_params=params(6),
        cost_estimate=small(),
        name="solve",
    )(col, *parts, *hops)


def stack(parts):
    size = parts[0].shape[0]

    def body(*refs):
        for k, ref in enumerate(refs[:-1]):
            refs[-1][k * size : (k + 1) * size, :] = ref[...]

    return pl.pallas_call(
        body,
        in_specs=[VMEM] * len(parts),
        out_specs=VMEM,
        out_shape=shape(len(parts) * size, PANEL),
        compiler_params=params(4),
        cost_estimate=small(),
        name="stack",
    )(*parts)


def subtract(row, matrix, halves, mine, other, pairs):
    rows, width = matrix.shape
    tiles = 12
    size = rows // tiles
    block = width // (2 * pairs)

    def body(row_ref, a, p, mine_ref, other_ref, out, coeffs, ct, held, sems):
        chip, first = row_ref[0] // 2, row_ref[0] % 2 == 0
        for k in range(pairs):
            here = pl.ds(pl.multiple_of((chip ^ k) * block, block), block)
            one, two = mine_ref[here, :], other_ref[here, :]
            coeffs[2 * k * block : (2 * k + 1) * block, :] = jnp.where(first, one, two)
            coeffs[(2 * k + 1) * block : (2 * k + 2) * block, :] = jnp.where(first, two, one)
        ct_high, ct_low = split(coeffs[...].T)
        ct[:PANEL, :] = ct_high
        ct[PANEL : 2 * PANEL, :] = ct_high
        ct[2 * PANEL :, :] = ct_low
        copies = [
            pltpu.make_async_copy(held.at[t], out.at[pl.ds(t * size, size), :], sems.at[t])
            for t in range(tiles)
        ]
        for t in range(tiles):
            here = slice(t * size, (t + 1) * size)
            both = p[here, :]
            thrice = jnp.concatenate([both, both[:, :PANEL]], axis=1)
            value = a[here, :] - dot(thrice, ct[...], ((1,), (0,)))
            held[t] = value
            copies[t].start()
        for copy in copies:
            copy.wait()

    return pl.pallas_call(
        body,
        in_specs=[SMEM] + [VMEM] * 4,
        out_specs=ANY,
        out_shape=shape(rows, width),
        scratch_shapes=[
            pltpu.VMEM((width, PANEL), F32),
            pltpu.VMEM((3 * PANEL, width), BF16),
            pltpu.VMEM((tiles, size, width), F32),
            pltpu.SemaphoreType.DMA((tiles,)),
        ],
        compiler_params=params(22),
        cost_estimate=small(),
        name="subtract",
    )(row, matrix, halves, mine, other)


def program(n_row, n_col):
    pairs = n_row // 2

    def swap(x, bit):
        return lax.ppermute(x, "row", [(r, r ^ bit) for r in range(n_row)])

    def scatter(row, keep, give):
        parts = spread(row, keep, swap(give, 1), pairs)
        return [parts[0]] + [swap(parts[j], 2 * j) for j in reversed(range(1, pairs))]

    def shards(matrix):
        col = lax.axis_index("col").astype(jnp.int32).reshape(1)
        row = lax.axis_index("row").astype(jnp.int32).reshape(1)
        blocks = PANEL // BLOCK
        rows = matrix.shape[0] // CHUNKS
        shifts = CHUNKS + 1 + LAG * (n_col - 2)
        last = CHUNKS - 1 + LAG * (n_col - 1)
        first = LAG + 3
        due = [first + i * (CHUNKS - 1 - first) // (blocks - 1) for i in range(blocks)]
        sent, received, sums = [], [], {}
        half = state = packed = None
        for s in range(shifts + LAG):
            if s < LAG:
                sent.append(matrix[s * rows : (s + 1) * rows, :PANEL])
            elif s < shifts:
                after = [sums[s - 2 * LAG][0]] if s - 2 * LAG in sums else []
                if s == LAG:
                    keep, give = gram_part(col, row, matrix)
                    half = add([keep, swap(give, 1)])
                elif state is not None:
                    after.append(state[0])
                x = received[s - LAG]
                if s < CHUNKS:
                    sent.append(fill(col, x, matrix, s * rows, *after))
                elif s == CHUNKS:
                    sent.append(fill(col, x, packed, 0, *after))
                else:
                    sent.append(gate(x, *after))
            else:
                sent.append(received[s - LAG])
            if s < shifts:
                hops = [(h, h + 1) for h in range(n_col - 1) if 0 <= s - LAG * h <= CHUNKS]
                x = sent[s]
                if s == shifts - 1 and n_col > 2:
                    x = cut(col, x, n_col - 2)
                received.append(lax.ppermute(x, "col", hops))
            if LAG <= s <= last:
                before = sums[s - 1] if s > LAG else ()
                sums[s] = consume(
                    col, row, matrix, sent[s], s, before, pairs if s == last else 0
                )
            if s == LAG + 1:
                half = gate(half, received[0])
                state = [add([half] + [swap(half, 2 * j) for j in range(1, pairs)])]
            elif s == LAG + 2:
                mine = gate(state[0], sent[s])
                state = [mine, swap(mine, 1)]
            elif s in due:
                block = due.index(s)
                state = eliminate(col, row, [gate(state[0], sent[s]), *state[1:]], block)
                if block == blocks - 1:
                    state, packed = [state[0]], state[1]
                else:
                    state = [state]
        keep, give, halves = sums[last]
        parts = scatter(row, keep, give)
        inverse = [sent[CHUNKS + LAG * h] for h in range(n_col)]
        top_rows, coeffs = solve(col, parts, inverse)
        far = [swap(coeffs, 2 * j) for j in reversed(range(1, pairs))]
        mine = stack([coeffs] + far[::-1])
        return top_rows, subtract(row, matrix, halves, mine, swap(mine, 1), pairs)

    return shards


def solution(mesh):
    return jax.shard_map(
        program(mesh.shape["row"], mesh.shape["col"]),
        mesh=mesh,
        in_specs=(P("row", "col"),),
        out_specs=(P(("col", "row"), None), P("row", "col")),
        check_vma=False,
    )
```

```python
import jax
import jax.numpy as jnp
from jax import lax
from jax.experimental import pallas as pl
from jax.experimental.pallas import tpu as pltpu
from jax.sharding import PartitionSpec as P

PANEL = 256
CHUNKS = 16
LAG = 3
HALF = PANEL // 2
QUARTER = PANEL // 4
PACKED = 2 * QUARTER + QUARTER // 2
OWN = 4
BLOCK = 32
HIGHEST = lax.Precision.HIGHEST
F32, BF16 = jnp.float32, jnp.bfloat16
ANY = pl.BlockSpec(memory_space=pl.ANY)
SMEM = pl.BlockSpec(memory_space=pltpu.SMEM)
VMEM = pl.BlockSpec(memory_space=pltpu.VMEM)


def params(mib):
    return pltpu.CompilerParams(vmem_limit_bytes=mib * 1024 * 1024)


def small():
    return pl.CostEstimate(flops=1, bytes_accessed=1, transcendentals=0)


def shape(*dims, dtype=F32):
    return jax.ShapeDtypeStruct(dims, dtype)


def split(x):
    hi = x.astype(BF16)
    return hi, (x - hi.astype(F32)).astype(BF16)


def dot(a, b, dims, precision=None):
    return lax.dot_general(
        a, b, (dims, ((), ())), precision=precision, preferred_element_type=F32
    )


def gate(x, *after):
    def body(*refs):
        pass

    return pl.pallas_call(
        body,
        in_specs=[ANY] * (1 + len(after)),
        out_specs=ANY,
        out_shape=shape(*x.shape, dtype=x.dtype),
        input_output_aliases={0: 0},
        compiler_params=params(1),
        cost_estimate=small(),
        name="gate",
    )(x, *after)


def fill(col, received, source, first, *after):
    rows = min(received.shape[0], source.shape[0] - first)

    def body(col_ref, _, source_ref, *refs):
        out, sem = refs[-2:]

        @pl.when(col_ref[0] == 0)
        def _():
            own = source_ref.at[pl.ds(first, rows), pl.ds(0, PANEL)]
            copy = pltpu.make_async_copy(own, out.at[pl.ds(0, rows), :], sem)
            copy.start()
            copy.wait()

    return pl.pallas_call(
        body,
        in_specs=[SMEM] + [ANY] * (2 + len(after)),
        out_specs=ANY,
        out_shape=shape(*received.shape),
        input_output_aliases={1: 0},
        scratch_shapes=[pltpu.SemaphoreType.DMA(())],
        compiler_params=params(1),
        cost_estimate=small(),
        name="fill",
    )(col, received, source, *after)


def halve(total, row_ref, keep, give, pairs):
    size = total.shape[0] // (2 * pairs)
    core = row_ref[0] % 2
    for k in range(pairs):
        here = slice(k * size, (k + 1) * size)
        mine = pl.multiple_of((2 * k + core) * size, size)
        other = pl.multiple_of((2 * k + 1 - core) * size, size)
        keep[here, :] = total[pl.ds(mine, size), :]
        give[here, :] = total[pl.ds(other, size), :]


def spread(row, keep, got, pairs):
    size = keep.shape[0] // pairs

    def body(row_ref, keep_ref, got_ref, *outs):
        chip = row_ref[0] // 2
        for j, out in enumerate(outs):
            here = pl.ds(pl.multiple_of((chip ^ j) * size, size), size)
            out[...] = keep_ref[here, :] + got_ref[here, :]

    return pl.pallas_call(
        body,
        in_specs=[SMEM, VMEM, VMEM],
        out_specs=(VMEM,) * pairs,
        out_shape=(shape(size, PANEL),) * pairs,
        compiler_params=params(4),
        cost_estimate=small(),
        name="spread",
    )(row, keep, got)


def add(parts):
    def body(*refs):
        total = refs[0][...]
        for ref in refs[1:-1]:
            total += ref[...]
        refs[-1][...] = total

    return pl.pallas_call(
        body,
        in_specs=[VMEM] * len(parts),
        out_specs=VMEM,
        out_shape=shape(*parts[0].shape),
        compiler_params=params(2),
        cost_estimate=small(),
        name="add",
    )(*parts)


def gram_part(col, row, matrix):
    tiles = 8
    rows = matrix.shape[0] // tiles

    def body(col_ref, row_ref, source, keep, give, held, sems):
        @pl.when(col_ref[0] == 0)
        def _():
            copies = [
                pltpu.make_async_copy(
                    source.at[pl.ds(t * rows, rows), pl.ds(0, PANEL)], held.at[t], sems.at[t]
                )
                for t in range(tiles)
            ]
            for copy in copies:
                copy.start()
            square = jnp.zeros((PANEL, PANEL), F32)
            cross = jnp.zeros((PANEL, PANEL), F32)
            dims = ((0,), (0,))
            for t in range(tiles):
                copies[t].wait()
                high, low = split(held[t])
                square += dot(high, high, dims) + dot(low, low, dims)
                cross += dot(high, low, dims)
            total = square + (cross + cross.T)
            upper = row_ref[0] % 2 == 0
            keep[...] = jnp.where(upper, total[:HALF, :], total[HALF:, :])
            give[...] = jnp.where(upper, total[HALF:, :], total[:HALF, :])

    return pl.pallas_call(
        body,
        in_specs=[SMEM, SMEM, ANY],
        out_specs=(VMEM, VMEM),
        out_shape=(shape(HALF, PANEL),) * 2,
        scratch_shapes=[
            pltpu.VMEM((tiles, rows, PANEL), F32),
            pltpu.SemaphoreType.DMA((tiles,)),
        ],
        compiler_params=params(53),
        cost_estimate=small(),
        name="gram",
    )(col, row, matrix)


def eliminate(col, row, state, block):
    first, last = block * BLOCK, (block + 1) * BLOCK
    width = 2 * PANEL

    def body(col_ref, row_ref, src, *rest):
        out, packed = (rest[-2:] if last == PANEL else (rest[-1], None))

        @pl.when(col_ref[0] == 0)
        def _():
            if block == 0:
                row = lax.broadcasted_iota(jnp.int32, (PANEL, PANEL), 0)
                lane = lax.broadcasted_iota(jnp.int32, (PANEL, PANEL), 1)
                upper = row_ref[0] % 2 == 0
                out[:HALF, :PANEL] = jnp.where(upper, src[...], rest[0][...])
                out[HALF:, :PANEL] = jnp.where(upper, rest[0][...], src[...])
                out[:, PANEL:] = (row == lane).astype(F32)
            else:
                out[...] = src[...]
            row = lax.broadcasted_iota(jnp.int32, (BLOCK, BLOCK), 0)
            lane = lax.broadcasted_iota(jnp.int32, (BLOCK, BLOCK), 1)
            work = jnp.concatenate(
                [out[first:last, first:last], (row == lane).astype(F32)], axis=1
            )
            below = lax.broadcasted_iota(jnp.int32, (BLOCK, 2 * BLOCK), 0)
            scale = jnp.zeros((BLOCK, 2 * BLOCK), F32)
            for i in range(0, BLOCK, 2):
                column = jnp.broadcast_to(work[:, i : i + 1], work.shape)
                follow = jnp.broadcast_to(work[:, i + 1 : i + 2], work.shape)
                upper, lower = work[i : i + 1, :], work[i + 1 : i + 2, :]
                pivot, cross = column[i : i + 1, :], column[i + 1 : i + 2, :]
                inverse = 1.0 / pivot
                ratio = cross * inverse
                second = follow[i + 1 : i + 2, :] - ratio * follow[i : i + 1, :]
                factor = jnp.where(below > i, column * inverse, 0.0)
                follow = follow - factor * follow[i : i + 1, :]
                after = jnp.where(below > i + 1, follow * (1.0 / second), 0.0)
                lower = lower - ratio * upper
                work = work - factor * upper - after * lower
                scale = jnp.where(below == i, pivot, jnp.where(below == i + 1, second, scale))
            root = lax.rsqrt(scale)
            root = root * (1.5 - 0.5 * scale * root * root)
            rows = dot((work * root)[:, BLOCK:], out[first:last, :], ((1,), (0,)), HIGHEST)
            out[first:last, :] = rows
            if last == PANEL:
                q = QUARTER
                packed[:q, :] = out[3 * q :, PANEL:]
                packed[q : 2 * q, : 3 * q] = out[2 * q : 3 * q, PANEL : PANEL + 3 * q]
                packed[q : 2 * q, 3 * q :] = out[:q, PANEL : PANEL + q]
                for k in range(4):
                    high, left = q + k % 2 * (q // 2), PANEL + k // 2 * q
                    packed[2 * q :, k * q : (k + 1) * q] = out[high : high + q // 2, left : left + q]
            else:
                left, right = last // 128 * 128, PANEL + -(-last // 128) * 128
                out[last:, left:right] -= dot(
                    rows[:, last:PANEL], rows[:, left:right], ((0,), (0,)), HIGHEST
                )

    return pl.pallas_call(
        body,
        in_specs=[SMEM, SMEM] + [VMEM] * len(state),
        out_specs=(VMEM, VMEM) if last == PANEL else VMEM,
        out_shape=(shape(PANEL, width), shape(PACKED, PANEL))
        if last == PANEL
        else shape(PANEL, width),
        input_output_aliases={2: 0} if block else {},
        compiler_params=params(8),
        cost_estimate=small(),
        name=f"eliminate{block}",
    )(col, row, *state)


def consume(col, row, matrix, sent, step, before, pairs):
    rows, width = sent.shape[0], matrix.shape[1]

    def body(col_ref, row_ref, block, source, *refs):
        if pairs:
            total, _, keep, give, halves, held, sem, summed, turned = refs
        elif step > LAG:
            total, _, out, halves, held, sem = refs
        else:
            out, halves, held, sem = refs
        chunk = step - LAG * col_ref[0]

        def part(first, piece):
            count = piece.shape[0]
            here = pl.ds(pl.multiple_of(first, rows), count)
            high, low = split(piece)
            held[:count, :PANEL] = high
            held[:count, PANEL:] = low
            copy = pltpu.make_async_copy(held.at[pl.ds(0, count), :], halves.at[here, :], sem)
            copy.start()
            a_high, a_low = split(block[here, :])
            dims = ((0,), (0,))
            value = dot(high, a_high, dims) + dot(low, a_high, dims) + dot(high, a_low, dims)
            copy.wait()
            return value

        valid = (col_ref[0] > 0) & (chunk >= 0) & (chunk < CHUNKS)
        if pairs:
            summed[...] = total[...]

            @pl.when(valid)
            def _():
                summed[...] += part(chunk * rows, source[...])

            turned[...] = summed[...].T
            halve(turned, row_ref, keep, give, pairs)
        else:
            out[...] = total[...] if step > LAG else jnp.zeros_like(out)

            @pl.when(valid)
            def _():
                out[...] += part(chunk * rows, source[...])

            if step == CHUNKS + 1:

                @pl.when(col_ref[0] == 0)
                def _():
                    size = OWN * rows

                    @pl.loop(0, CHUNKS // OWN)
                    def _(k):
                        here = pl.ds(pl.multiple_of(k * size, size), size)
                        out[...] += part(k * size, block[here, :PANEL])

    halves = shape(matrix.shape[0], 2 * PANEL, dtype=BF16)
    if pairs:
        outs = (shape(width // 2, PANEL),) * 2 + (halves,)
    else:
        outs = (shape(PANEL, width), halves)
    return pl.pallas_call(
        body,
        in_specs=[SMEM, SMEM, VMEM, VMEM] + ([VMEM, ANY] if step > LAG else []),
        out_specs=(VMEM,) * (len(outs) - 1) + (ANY,),
        out_shape=outs,
        input_output_aliases={5: len(outs) - 1} if step > LAG else {},
        scratch_shapes=[
            pltpu.VMEM((OWN * rows if step == CHUNKS + 1 else rows, 2 * PANEL), BF16),
            pltpu.SemaphoreType.DMA(()),
        ]
        + ([pltpu.VMEM(dims, F32) for dims in ((PANEL, width), (width, PANEL))] if pairs else []),
        compiler_params=params(16),
        cost_estimate=small(),
        name="consume",
    )(col, row, matrix, sent, *before)


def cut(col, x, where):
    def body(col_ref, source, out):
        @pl.when(col_ref[0] == where)
        def _():
            out[...] = source[:PACKED, :]

    return pl.pallas_call(
        body,
        in_specs=[SMEM, VMEM],
        out_specs=VMEM,
        out_shape=shape(PACKED, PANEL),
        compiler_params=params(2),
        cost_estimate=small(),
        name="cut",
    )(col, x)


def solve(col, parts, hops):
    n, rows = len(parts), parts[0].shape[0]

    def body(col_ref, *refs):
        sources, (top, coeffs, inverse) = refs[n:-3], refs[-3:]
        q = QUARTER
        inverse[:HALF, HALF:] = jnp.zeros((HALF, HALF), F32)
        inverse[:q, q:HALF] = jnp.zeros((q, q), F32)
        inverse[HALF : 3 * q, 3 * q :] = jnp.zeros((q, q), F32)
        for h, source in enumerate(sources):

            @pl.when(col_ref[0] == h)
            def _():
                inverse[3 * q :, :] = source[:q, :]
                inverse[2 * q : 3 * q, : 3 * q] = source[q : 2 * q, : 3 * q]
                inverse[:q, :q] = source[q : 2 * q, 3 * q :]
                for k in range(4):
                    high, left = q + k % 2 * (q // 2), k // 2 * q
                    piece = source[2 * q : PACKED, k * q : (k + 1) * q]
                    inverse[high : high + q // 2, left : left + q] = piece

        total = refs[0][...]
        for ref in refs[1:n]:
            total += ref[...]
        value = dot(total, inverse[...], ((1,), (1,)), HIGHEST)
        top[...] = value
        coeffs[...] = dot(value, inverse[...], ((1,), (0,)), HIGHEST)

    return pl.pallas_call(
        body,
        in_specs=[SMEM] + [VMEM] * (n + len(hops)),
        out_specs=(VMEM, VMEM),
        out_shape=(shape(rows, PANEL),) * 2,
        scratch_shapes=[pltpu.VMEM((PANEL, PANEL), F32)],
        compiler_params=params(6),
        cost_estimate=small(),
        name="solve",
    )(col, *parts, *hops)


def stack(parts):
    size = parts[0].shape[0]

    def body(*refs):
        for k, ref in enumerate(refs[:-1]):
            refs[-1][k * size : (k + 1) * size, :] = ref[...]

    return pl.pallas_call(
        body,
        in_specs=[VMEM] * len(parts),
        out_specs=VMEM,
        out_shape=shape(len(parts) * size, PANEL),
        compiler_params=params(4),
        cost_estimate=small(),
        name="stack",
    )(*parts)


def subtract(row, matrix, halves, mine, other, pairs):
    rows, width = matrix.shape
    tiles = 12
    size = rows // tiles
    block = width // (2 * pairs)

    def body(row_ref, a, p, mine_ref, other_ref, out, coeffs, ct, held, sems):
        chip, first = row_ref[0] // 2, row_ref[0] % 2 == 0
        for k in range(pairs):
            here = pl.ds(pl.multiple_of((chip ^ k) * block, block), block)
            one, two = mine_ref[here, :], other_ref[here, :]
            coeffs[2 * k * block : (2 * k + 1) * block, :] = jnp.where(first, one, two)
            coeffs[(2 * k + 1) * block : (2 * k + 2) * block, :] = jnp.where(first, two, one)
        ct_high, ct_low = split(coeffs[...].T)
        ct[:PANEL, :] = ct_high
        ct[PANEL : 2 * PANEL, :] = ct_high
        ct[2 * PANEL :, :] = ct_low
        copies = [
            pltpu.make_async_copy(held.at[t], out.at[pl.ds(t * size, size), :], sems.at[t])
            for t in range(tiles)
        ]
        for t in range(tiles):
            here = slice(t * size, (t + 1) * size)
            both = p[here, :]
            thrice = jnp.concatenate([both, both[:, :PANEL]], axis=1)
            value = a[here, :] - dot(thrice, ct[...], ((1,), (0,)))
            held[t] = value
            copies[t].start()
        for copy in copies:
            copy.wait()

    return pl.pallas_call(
        body,
        in_specs=[SMEM] + [VMEM] * 4,
        out_specs=ANY,
        out_shape=shape(rows, width),
        scratch_shapes=[
            pltpu.VMEM((width, PANEL), F32),
            pltpu.VMEM((3 * PANEL, width), BF16),
            pltpu.VMEM((tiles, size, width), F32),
            pltpu.SemaphoreType.DMA((tiles,)),
        ],
        compiler_params=params(22),
        cost_estimate=small(),
        name="subtract",
    )(row, matrix, halves, mine, other)


def program(n_row, n_col):
    pairs = n_row // 2

    def swap(x, bit):
        return lax.ppermute(x, "row", [(r, r ^ bit) for r in range(n_row)])

    def scatter(row, keep, give):
        parts = spread(row, keep, swap(give, 1), pairs)
        return [parts[0]] + [swap(parts[j], 2 * j) for j in reversed(range(1, pairs))]

    def shards(matrix):
        col = lax.axis_index("col").astype(jnp.int32).reshape(1)
        row = lax.axis_index("row").astype(jnp.int32).reshape(1)
        blocks = PANEL // BLOCK
        rows = matrix.shape[0] // CHUNKS
        shifts = CHUNKS + 1 + LAG * (n_col - 2)
        last = CHUNKS - 1 + LAG * (n_col - 1)
        first = LAG + 3
        due = [first + i * (CHUNKS - 1 - first) // (blocks - 1) for i in range(blocks)]
        sent, received, sums = [], [], {}
        half = state = packed = None
        for s in range(shifts + LAG):
            if s < LAG:
                sent.append(matrix[s * rows : (s + 1) * rows, :PANEL])
            elif s < shifts:
                after = [sums[s - LAG - 1][0]] if s - LAG - 1 in sums else []
                if s == LAG:
                    keep, give = gram_part(col, row, matrix)
                    half = add([keep, swap(give, 1)])
                elif state is not None:
                    after.append(state[0])
                x = received[s - LAG]
                if s < CHUNKS:
                    sent.append(fill(col, x, matrix, s * rows, *after))
                elif s == CHUNKS:
                    sent.append(fill(col, x, packed, 0, *after))
                else:
                    sent.append(gate(x, *after))
            else:
                sent.append(received[s - LAG])
            if s < shifts:
                hops = [(h, h + 1) for h in range(n_col - 1) if 0 <= s - LAG * h <= CHUNKS]
                x = sent[s]
                if s == shifts - 1 and n_col > 2:
                    x = cut(col, x, n_col - 2)
                received.append(lax.ppermute(x, "col", hops))
            if LAG <= s <= last:
                before = sums[s - 1] if s > LAG else ()
                sums[s] = consume(
                    col, row, matrix, sent[s], s, before, pairs if s == last else 0
                )
            if s == LAG + 1:
                half = gate(half, received[0])
                state = [add([half] + [swap(half, 2 * j) for j in range(1, pairs)])]
            elif s == LAG + 2:
                mine = gate(state[0], sent[s])
                state = [mine, swap(mine, 1)]
            elif s in due:
                block = due.index(s)
                state = eliminate(col, row, [gate(state[0], sent[s]), *state[1:]], block)
                if block == blocks - 1:
                    state, packed = [state[0]], state[1]
                else:
                    state = [state]
        keep, give, halves = sums[last]
        parts = scatter(row, keep, give)
        inverse = [sent[CHUNKS + LAG * h] for h in range(n_col)]
        top_rows, coeffs = solve(col, parts, inverse)
        far = [swap(coeffs, 2 * j) for j in reversed(range(1, pairs))]
        mine = stack([coeffs] + far[::-1])
        return top_rows, subtract(row, matrix, halves, mine, swap(mine, 1), pairs)

    return shards


def solution(mesh):
    return jax.shard_map(
        program(mesh.shape["row"], mesh.shape["col"]),
        mesh=mesh,
        in_specs=(P("row", "col"),),
        out_specs=(P(("col", "row"), None), P("row", "col")),
        check_vma=False,
    )
```
